128 devices in a mesh: front: 32 (over z, y, core), blk: 4 (over x).
Axes of the slice: x: 4, y: 4, z: 4, core: 2. Of those that a mesh axis runs over, the one named last changes fastest.
Arguments:
- root_tiles: bfloat16 [32, 5, 640, 10240], P('front', None, None, 'blk'), as said below
- child_tiles: bfloat16 [32, 3, 256, 4096], P('front', None, None, 'blk'), as said below
- child_update: bfloat16 [49152, 2, 4096], P('front', None, 'blk'), may hold values from -0.0625 to 0.0625
- extend_map: int32 [384], P('front'), may hold values from 0 to 319, as said below
- root_side: float32 [32, 2, 24, 640], P('front'), may hold values from -6 to 6
- child_side: float32 [32, 2, 24, 256], P('front'), may hold values from -6 to 6
Outputs:
- root_field: float32 [32, 2, 24, 640], P('front')
- child_field: float32 [32, 2, 24, 256], P('front')
The draws below stay inside these ranges and needn't reach their ends.
Inputs may be any that keep to these rules, and one draw needn't show every extreme that they name: `extend_map`: within one child the 192 blocks name distinct root blocks. Root block r lies in panel k = r div (80) and stripe q = (r mod (80)) div (5) and is held by front index 16 * min(k, 3 - k) + q. The 12 entries held by one front index name at most 1 root blocks held by any one front index, and exactly 1 for some. `root_tiles`: diagonal slots are upper triangular with diagonal entries between 0.75 and 1.25. `child_tiles`: diagonal slots are upper triangular with diagonal entries between 0.75 and 1.25.
All inputs are finite; a program needn't handle non-finite values.
Results may differ from the reference program's by a relative error of at most 0.0003.
Values sent between devices are 32-bit elements; how exact they have to be, the bound alone decides.
A program may use at most 128 MiB of HBM per device.

```python
import math
import jax
import jax.numpy as jnp
from jax import lax

ROOT_ORDER = 40960
CHILD_PIVOT = 8192
CHILD_UPDATE = 24576
DIRECTIONS = 24
BLOCK_ROWS = 128
ROOT_PANELS = 4
CHILD_PANELS = 2
ROW_SPLIT = 16
ROOT_STRIPE = 640
CHILD_PANEL = 4096
CHILD_STRIPE = 256
N_FRONT = 32


def factor_draw(key, devices, group_size, split, panels, stripe_rows, order):
    width = split * stripe_rows
    slot_count = panels + 1

    def one_device(device_index):
        values = jax.random.normal(jax.random.fold_in(key, device_index), (slot_count, stripe_rows, width), jnp.float32)
        slot_index = jnp.arange(slot_count)[:, None, None]
        row_index = device_index % split * stripe_rows + jnp.arange(stripe_rows)[None, :, None]
        col_index = jnp.arange(width)[None, None, :]
        pair_index = device_index % group_size // split
        diagonal = (slot_index == pair_index) | (slot_index == panels)
        upper_part = jnp.where(col_index > row_index, 0.5 * values / math.sqrt(width), 0.0)
        upper_part = jnp.where(col_index == row_index, 1.0 + 0.25 * jnp.tanh(values), upper_part)
        lower_part = values / math.sqrt(order)
        return jnp.where(diagonal, upper_part, lower_part).astype(jnp.bfloat16)
    return lax.map(one_device, jnp.arange(devices))


def draw_root_tiles(key, part):
    key = jax.random.fold_in(key, 1)
    return factor_draw(key, 2 * ROW_SPLIT, 2 * ROW_SPLIT, ROW_SPLIT, ROOT_PANELS, ROOT_STRIPE, ROOT_ORDER)


def draw_child_tiles(key, part):
    key = jax.random.fold_in(key, 2)
    return factor_draw(key, 2 * ROW_SPLIT, ROW_SPLIT, ROW_SPLIT, CHILD_PANELS, CHILD_STRIPE, CHILD_PIVOT)


def draw_extend_map(key, part):
    key = jax.random.fold_in(key, 3)
    devices = 2 * ROW_SPLIT
    slot_count = ROOT_ORDER // (BLOCK_ROWS * devices)
    send_count = 2 * CHILD_UPDATE // (BLOCK_ROWS * devices)
    stripe_blocks = slot_count // 2
    half_count = devices // 2
    pieces = []
    for child_index in range(2):
        perm_key, shift_key = jax.random.split(jax.random.fold_in(key, child_index + 1))
        scores = jax.random.randint(perm_key, (devices,), 0, 4096) * devices + jnp.arange(devices)
        shifts = jax.random.randint(shift_key, (devices,), 0, slot_count)
        ordering = jnp.argsort(scores, stable=True)
        source_dev = jnp.arange(half_count)[:, None]
        block_index = jnp.arange(send_count)[None, :]
        global_index = source_dev * send_count + block_index
        route_index = global_index % devices
        ident = global_index // devices
        owner_dev = ordering[route_index]
        slot_place = (ident + shifts[route_index]) % slot_count
        pair_index = owner_dev // ROW_SPLIT
        stripe_index = owner_dev % ROW_SPLIT
        second_half = slot_place // stripe_blocks
        within_block = slot_place % stripe_blocks
        column_index = jnp.where(second_half == 0, pair_index, ROOT_PANELS - 1 - pair_index)
        flat = column_index * ROW_SPLIT * stripe_blocks + stripe_index * stripe_blocks + within_block
        pieces.append(flat.reshape(-1))
    return jnp.concatenate(pieces).astype(jnp.int32)


def steps_of(own_key, dims, shards, least, top_value):
    loudness = 1.0
    for dim, shards_of in shards:
        steps = jax.random.uniform(jax.random.fold_in(jax.random.fold_in(own_key, 6), dim), (shards_of,), jnp.float32, least / len(shards), top_value / len(shards))
        loudness = loudness * jnp.repeat(jnp.exp(steps), dims[dim] // shards_of).reshape((-1,) + (1,) * (len(dims) - 1 - dim))
    return loudness


def noise(key, dims, scale, reach, cuts=(), kind=jnp.bfloat16):
    values = jax.random.normal(key, dims, jnp.float32) * scale
    if len(cuts) > 0:
        values = steps_of(key, dims, cuts, -0.22, 0.18) * values
    return jnp.clip(values, min=-reach, max=reach).astype(kind)


def setup_inputs(seed: int = 0) -> dict:
    streams_of = jax.random.split(jax.random.key(seed), 7)
    root_tiles = draw_root_tiles(jax.random.fold_in(streams_of[6], 71), 0)
    child_tiles = draw_child_tiles(jax.random.fold_in(streams_of[6], 71), 0)
    child_update = noise(streams_of[2], (2 * CHILD_UPDATE, CHILD_PANELS, CHILD_PANEL), CHILD_PIVOT ** -0.5, 0.0625, ((0, 32), (2, 4)))
    extend_map = draw_extend_map(jax.random.fold_in(streams_of[6], 71), 0)
    root_side = noise(streams_of[4], (N_FRONT, 2, DIRECTIONS, ROOT_STRIPE), 1.0, 6.0, ((0, 32),), jnp.float32)
    child_side = noise(streams_of[5], (N_FRONT, 2, DIRECTIONS, CHILD_STRIPE), 1.0, 6.0, ((0, 32),), jnp.float32)
    return {"root_tiles": root_tiles, "child_tiles": child_tiles, "child_update": child_update, "extend_map": extend_map, "root_side": root_side, "child_side": child_side}


exact_mode = lax.Precision.HIGHEST


def multiply(left, right):
    return jnp.dot(left, right, precision=exact_mode)


def panel_owner(panels, column):
    lower = min(column, panels - 1 - column)
    second = 0 if column == lower else 1
    return lower, second


def full_tile(factor_tiles, first_device, split, panels, row_panel, col_panel):
    lower, second = panel_owner(panels, row_panel)
    slot_index = col_panel if second == 0 else lower + 1 + col_panel
    stripes = [factor_tiles[first_device + split * lower + stripe_index, slot_index] for stripe_index in range(split)]
    return jnp.concatenate(stripes, axis=0).astype(jnp.float32)


def panel_vector(packed, first_device, split, panels, column):
    lower, second = panel_owner(panels, column)
    stripes = [packed[first_device + split * lower + stripe_index, second] for stripe_index in range(split)]
    return jnp.concatenate(stripes, axis=1)


def pack_vectors(pieces, first_device, split, panels, target):
    stripe_rows = pieces[0].shape[1] // split
    for column in range(panels):
        lower, second = panel_owner(panels, column)
        for stripe_index in range(split):
            stripe = pieces[column][:, stripe_index * stripe_rows:(stripe_index + 1) * stripe_rows]
            target = target.at[first_device + split * lower + stripe_index, second].set(stripe)
    return target


def solve_forward(factor_tiles, packed, first_device, split, panels, extra):
    solved = []
    for column in range(panels):
        rest = panel_vector(packed, first_device, split, panels, column)
        if extra is not None:
            rest = rest - extra[column]
        for inner in range(column):
            rest = rest - multiply(solved[inner], full_tile(factor_tiles, first_device, split, panels, column, inner).T)
        solved.append(multiply(rest, full_tile(factor_tiles, first_device, split, panels, column, column)))
    return solved


def solve_backward(factor_tiles, solved, first_device, split, panels, extra):
    result = [None] * panels
    for column in reversed(range(panels)):
        rest = solved[column]
        if extra is not None:
            rest = rest - extra[column]
        for later in range(column + 1, panels):
            rest = rest - multiply(result[later], full_tile(factor_tiles, first_device, split, panels, later, column))
        result[column] = multiply(rest, full_tile(factor_tiles, first_device, split, panels, column, column).T)
    return result


def reference(root_tiles, child_tiles, child_update, extend_map, root_side, child_side):
    fronts = root_tiles.shape[0]
    half_count = fronts // 2
    split = fronts // 2
    root_panels = root_tiles.shape[1] - 1
    child_panels = child_tiles.shape[1] - 1
    directions = root_side.shape[2]
    updates = child_update.shape[0] // 2
    map_blocks = extend_map.shape[0] // 2
    child_solved = [solve_forward(child_tiles, child_side, child_index * half_count, split, child_panels, None) for child_index in range(2)]
    extra = jnp.zeros((directions, ROOT_ORDER), jnp.float32)
    row_lists = []
    for child_index in range(2):
        slab = child_update[child_index * updates:(child_index + 1) * updates]
        contribution = jnp.zeros((directions, updates), jnp.float32)
        for column in range(child_panels):
            contribution = contribution + multiply(child_solved[child_index][column], slab[:, column, :].astype(jnp.float32).T)
        blocks = extend_map[child_index * map_blocks:(child_index + 1) * map_blocks]
        rows = (blocks[:, None] * BLOCK_ROWS + jnp.arange(BLOCK_ROWS, dtype=jnp.int32)[None, :]).reshape(-1).astype(jnp.int32)
        row_lists.append(rows)
        extra = extra.at[:, rows].add(contribution)
    panel_width = ROOT_ORDER // root_panels
    root_extra = [extra[:, column * panel_width:(column + 1) * panel_width] for column in range(root_panels)]
    root_solved = solve_forward(root_tiles, root_side, 0, split, root_panels, root_extra)
    root_result = solve_backward(root_tiles, root_solved, 0, split, root_panels, None)
    root_natural = jnp.concatenate(root_result, axis=1)
    root_field = pack_vectors(root_result, 0, split, root_panels, jnp.zeros(root_side.shape, jnp.float32))
    child_field = jnp.zeros(child_side.shape, jnp.float32)
    for child_index in range(2):
        slab = child_update[child_index * updates:(child_index + 1) * updates]
        needed = root_natural[:, row_lists[child_index]]
        child_extra = [multiply(needed, slab[:, column, :].astype(jnp.float32)) for column in range(child_panels)]
        child_result = solve_backward(child_tiles, child_solved[child_index], child_index * half_count, split, child_panels, child_extra)
        child_field = pack_vectors(child_result, child_index * half_count, split, child_panels, child_field)
    return root_field, child_field
```

```python
import functools
import types

import jax
import jax.numpy as jnp
from jax import lax
from jax.experimental import pallas as pl
from jax.experimental.pallas import tpu as pltpu
from jax.sharding import PartitionSpec as P

LANES = 128
MESH = pl.DeviceIdType.MESH
ROOT_PANELS = 4

BACK_2, BACK_1, BACK_0, EARLY_1, EARLY_0 = 4, 5, 6, 7, 8
ROOT_SOURCES = (0, 1, 1, 0, 0, 1, 1, 0, 0)
ROOT_TARGETS = (None, None, 0, 0, 1, 1, 0)
ROOT_ROWS = (0, 1, 1, 0, 0, 1, 1, 0)
CHILD_SUMS, CHILD_ROWS = 4, 3


def loop(count, body, start=0):
    lax.fori_loop(start, count, lambda i, c: (body(i), c)[1], 0)


def wait_bytes(ref, sem):
    pltpu.make_async_copy(ref, ref, sem).wait()


def split(value):
    high = value.astype(jnp.bfloat16).astype(jnp.float32)
    return jnp.concatenate([high, value - high], axis=0).astype(jnp.bfloat16)


def lane_block(index, width=LANES):
    if isinstance(index, int):
        return pl.ds(index * width, width)
    return pl.ds(pl.multiple_of(index * width, width), width)


def put(dest, index, value):
    dest[:, lane_block(index)] = split(value)


def fold(product):
    half = product.shape[0] // 2
    return product[:half] + product[half:]


def kernel(
    fronts, blks,
    emap, rside, cside, rt_hbm, ct_hbm, gt_hbm, rout, cout,
    rt, ct, gt, run, xr, xv, xc, xvc, xn, pb, ob, ar, rk, ak, tgs, tgr, zb,
    rows_r, term_r, recv_r, y_r, rows_c, term_c, recv_c, y_c,
    own, place, inv,
    load_sem, blk_s, blk_r, rs_s, rs_r, ag_s, ag_r, x_s, x_r,
):
    f = lax.axis_index("front")
    b = lax.axis_index("blk")
    half = fronts // 2
    p = f // half
    q = f % half
    directions = rside.shape[1]
    g3 = directions // 8
    root_rb = rside.shape[2] // LANES
    child_rb = cside.shape[2] // LANES
    sends = pb.shape[0]

    def load(src, dst, index):
        return pltpu.make_async_copy(src, dst, load_sem.at[index])

    loads_c = [load(ct_hbm.at[i], ct.at[i], i) for i in range(3)]
    loads_g = [load(gt_hbm.at[i], gt.at[i], 3 + i) for i in range(2)]
    loads_r = [load(rt_hbm.at[i], rt.at[i], 5 + i) for i in range(ROOT_PANELS + 1)]
    for c in loads_c + loads_g + loads_r:
        c.start()

    barrier = pltpu.get_barrier_semaphore()
    loop(fronts, lambda i: pl.semaphore_signal(
        barrier, inc=1, device_id=((f + i) % fronts, b), device_id_type=MESH), 1)
    loop(blks, lambda i: pl.semaphore_signal(
        barrier, inc=1, device_id=(f, (b + i) % blks), device_id_type=MESH), 1)

    def remote(src, dst, ss, rs, device):
        pltpu.make_async_remote_copy(
            src_ref=src, dst_ref=dst, send_sem=ss, recv_sem=rs, device_id=device, device_id_type=MESH
        ).start()

    root = types.SimpleNamespace(
        rows=rows_r, term=term_r, recv=recv_r, y=y_r, blk0=0, rs0=0, ag0=0,
        chunks=term_r.shape[1] // 2, base=0, chunk=f, rb=root_rb)
    child = types.SimpleNamespace(
        rows=rows_c, term=term_c, recv=recv_c, y=y_c, blk0=len(ROOT_ROWS), rs0=len(ROOT_SOURCES),
        ag0=len(ROOT_TARGETS), chunks=term_c.shape[1] // 2, base=p * half, chunk=q, rb=child_rb)

    def mine(side):
        return side.chunk < side.chunks

    def send_rows(side, phase, i):
        ref = side.rows.at[phase, b, i]
        for d in range(1, blks):
            remote(ref, ref, blk_s.at[side.blk0 + phase], blk_r.at[side.blk0 + phase], (f, (b + d) % blks))

    def rows_product(x, tile, slot, i):
        w = tile[slot, pl.ds(pl.multiple_of(i * LANES, LANES), LANES), :]
        return fold(lax.dot_general(x, w, (((1,), (1,)), ((), ())), preferred_element_type=jnp.float32))

    def rows_out(side, phase, x_ref, tile, slot, base):
        def body(i):
            product = rows_product(x_ref[...], tile, slot, i)
            side.rows[phase, b, i] = base(i, product)
            send_rows(side, phase, i)
        loop(side.rb, body)

    def rows_in(side, phase, use):
        wait_bytes(side.rows.at[phase, pl.ds(0, blks - 1)], blk_r.at[side.blk0 + phase])
        for i in range(side.rb):
            total = side.rows[phase, 0, i]
            for s in range(1, blks):
                total = total + side.rows[phase, s, i]
            use(i, total)

    def send_chunk(side, phase, ch):
        owner = side.base + ch
        src = side.term.at[phase, pl.ds(2 * ch, 2)]

        @pl.when(owner == f)
        def _():
            side.recv[phase, q] = src[...]

        @pl.when(owner != f)
        def _():
            remote(src, side.recv.at[phase, q], rs_s.at[side.rs0 + phase], rs_r.at[side.rs0 + phase], (owner, b))

    def cols_out(side, phase, x_ref, tile, slot, add=False, send=True):
        width = min(2 * LANES, tile.shape[2])
        steps = tile.shape[2] // width
        per = width // LANES * g3 // 2

        def body(i):
            c = (i + q) % steps
            w = tile[slot, :, lane_block(c, width)]
            product = fold(jnp.dot(x_ref[...], w, preferred_element_type=jnp.float32))
            for j in range(width // LANES):
                at = pl.ds((c * (width // LANES) + j) * g3, g3)
                value = product[:, j * LANES:(j + 1) * LANES].reshape(g3, 8, LANES)
                if add:
                    value = value + side.term[phase, at]
                side.term[phase, at] = value
            if send:
                for j in range(per):
                    send_chunk(side, phase, c * per + j)
        loop(steps, body)

    def take(side, phase, source=None):
        sem = rs_r.at[side.rs0 + phase]

        def some(count):
            wait_bytes(side.recv.at[phase, pl.ds(0, count)], sem)
        if source is None:
            some(half - 1)
        else:
            pl.when(p == source)(lambda: some(half - 1))
            pl.when(p != source)(lambda: some(half))
        total = side.recv[phase, 0]
        for s in range(1, half):
            total = total + side.recv[phase, s]
        return total

    def spread(side, phase, value, target=None):
        at = pl.ds(2 * side.chunk, 2)
        ref = side.y.at[phase, at]
        side.y[phase, at] = value
        sems = (ag_s.at[side.ag0 + phase], ag_r.at[side.ag0 + phase])
        if side is child:
            loop(half, lambda i: remote(ref, ref, *sems, (side.base + (q + i) % half, b)), 1)
        elif target is None:
            loop(fronts, lambda i: remote(ref, ref, *sems, ((f + i) % fronts, b)), 1)
        else:
            def body(i):
                peer = target * half + (q + i) % half
                pl.when(peer != f)(lambda: remote(ref, ref, *sems, (peer, b)))
            loop(half, body)

    def gather(side, phase, dest):
        def some(count):
            wait_bytes(side.y.at[phase, pl.ds(0, 2 * count)], ag_r.at[side.ag0 + phase])
        pl.when(mine(side))(lambda: some(side.chunks - 1))
        pl.when(jnp.logical_not(mine(side)))(lambda: some(side.chunks))

        def body(c):
            put(dest, c, side.y[phase, pl.ds(c * g3, g3)].reshape(directions, LANES))
        loop(2 * side.chunks // g3, body)

    def own_y(side, phase):
        return side.y[phase, pl.ds(2 * side.chunk, 2)]

    def lanes(i):
        return slice(i * LANES, (i + 1) * LANES)

    lead = (b == 0).astype(jnp.float32)

    for i in range(child_rb):
        put(xc, i, cside[0, :, lanes(i)])

    panel_blocks = half * root_rb

    def route(s):
        r = emap[s]
        k = lax.div(r, panel_blocks)
        within = lax.rem(r, panel_blocks)
        low = jnp.minimum(k, ROOT_PANELS - 1 - k)
        own[s] = half * low + lax.div(within, root_rb)
        place[s] = jnp.where(k == low, 0, root_rb) + lax.rem(within, root_rb)
    loop(sends, route)

    def invert(u):
        index = jnp.int32(0)
        tag = jnp.int32(-1)
        for s in range(sends):
            match = own[s] == u
            index = jnp.where(match, s, index)
            tag = jnp.where(match, place[s], tag)
        inv[u] = index
        tgs[u] = jnp.full((8, LANES), tag, jnp.int32)
    loop(fronts, invert)

    pl.semaphore_wait(barrier, fronts - 1 + blks - 1)

    loads_c[0].wait()
    cols_out(child, 0, xc, ct, 0)

    tgr[f] = tgs[f]

    def send_tag(i):
        u = (f + i) % fronts
        remote(tgs.at[u], tgr.at[f], x_s.at[0], x_r.at[0], (u, b))
    loop(fronts, send_tag, 1)

    def child_step(phase, base=None):
        @pl.when(mine(child))
        def _():
            total = take(child, phase)
            if base is not None:
                total = own_y(child, base) - total
            spread(child, phase, total)

    child_step(0)
    loads_c[1].wait()
    loads_c[2].wait()
    gather(child, 0, xvc)
    for i in range(child_rb):
        run[0, i] = lead * cside[1, :, lanes(i)]
    rows_out(child, 0, xvc, ct, 1, lambda i, d: run[0, i] - d)

    loads_g[0].wait()
    loads_g[1].wait()

    def first_update(s):
        pb[s] = rows_product(xvc[...], gt, 0, s)
    loop(sends, first_update)

    rows_in(child, 0, lambda i, v: put(xc, i, v))
    cols_out(child, 1, xc, ct, 2)
    child_step(1)
    gather(child, 1, xvc)

    def second_update(s):
        pb[s] = pb[s] + rows_product(xvc[...], gt, 1, s)
    loop(sends, second_update)

    ar[f] = pb[inv[f]].reshape(g3, 8, LANES)

    def send_block(i):
        u = (f + i) % fronts
        ob[u] = pb[inv[u]].reshape(g3, 8, LANES)
        remote(ob.at[u], ar.at[f], x_s.at[1], x_r.at[1], (u, b))
    loop(fronts, send_block, 1)
    for l in loads_r:
        l.wait()
    wait_bytes(tgr.at[pl.ds(0, fronts - 1)], x_r.at[0])
    wait_bytes(ar.at[pl.ds(0, fronts - 1)], x_r.at[1])

    def land(u, totals):
        block = ar[u]
        tag = tgr[u][None]
        return tuple(t + jnp.where(tag == s, block, 0.0) for s, t in enumerate(totals))
    zero = jnp.zeros((g3, 8, LANES), jnp.float32)
    landed = lax.fori_loop(0, fronts, land, (zero,) * (2 * root_rb))
    for h in range(2):
        for i in range(root_rb):
            run[h, i] = lead * rside[h, :, lanes(i)] - landed[h * root_rb + i].reshape(directions, LANES)

    def on(pair, body):
        pl.when(p == pair)(body)

    def root_step(phase, out, base=None, early=None):
        @pl.when(mine(root))
        def _():
            total = take(root, phase, ROOT_SOURCES[phase])
            if early is not None:
                total = total + take(root, early, ROOT_SOURCES[early])
            if base is not None:
                total = own_y(root, base) - total
            spread(root, out, total, ROOT_TARGETS[out])

    def from_run(h):
        return lambda i, d: run[h, i] - d

    def subtract(slot):
        def body(i):
            run[1, i] = run[1, i] - rows_product(xv[...], rt, slot, i)
        loop(root_rb, body)

    def solve_rows(phase, slot):
        rows_in(root, phase, lambda i, v: put(xr, i, v))
        cols_out(root, phase, xr, rt, slot)

    def finish_rows(phase, h):
        def use(i, v):
            zb[h * root_rb + i] = v.reshape(g3, 8, LANES)
            rout[h, :, lanes(i)] = v
            put(xr, i, v)
        rows_in(root, phase, use)

    @functools.partial(on, 0)
    def _():
        def body(i):
            rows_r[0, b, i] = run[0, i]
            send_rows(root, 0, i)
        loop(root_rb, body)
        solve_rows(0, 0)
    root_step(0, 0)
    gather(root, 0, xv)

    @functools.partial(on, 1)
    def _():
        rows_out(root, 1, xv, rt, 0, from_run(0))
        subtract(2)
        solve_rows(1, 1)

    on(0, lambda: subtract(1))
    root_step(1, 1)
    gather(root, 1, xv)

    @functools.partial(on, 1)
    def _():
        rows_out(root, 2, xv, rt, 3, from_run(1))
        solve_rows(2, 4)

    on(0, lambda: subtract(2))
    root_step(2, 2)

    @functools.partial(on, 0)
    def _():
        gather(root, 2, xv)
        rows_out(root, 3, xv, rt, 3, from_run(1))
        solve_rows(3, 4)
    root_step(3, 3)

    @functools.partial(on, 0)
    def _():
        gather(root, 3, xv)
        rows_out(root, 4, xv, rt, 4, lambda i, d: d)
        finish_rows(4, 1)
        cols_out(root, BACK_2, xr, rt, 3)
    root_step(BACK_2, 4, base=2)

    @functools.partial(on, 0)
    def _():
        cols_out(root, EARLY_1, xr, rt, 2)
        cols_out(root, EARLY_0, xr, rt, 1)

    @functools.partial(on, 1)
    def _():
        gather(root, 4, xv)
        rows_out(root, 5, xv, rt, 4, lambda i, d: d)
        finish_rows(5, 1)
        cols_out(root, BACK_1, xr, rt, 3)
    root_step(BACK_1, 5, base=1, early=EARLY_1)

    @functools.partial(on, 1)
    def _():
        cols_out(root, BACK_0, xr, rt, 2, send=False)
        gather(root, 5, xv)
        rows_out(root, 6, xv, rt, 1, lambda i, d: d)
        finish_rows(6, 0)
        cols_out(root, BACK_0, xr, rt, 0, add=True)
    root_step(BACK_0, 6, base=0, early=EARLY_0)

    @functools.partial(on, 0)
    def _():
        gather(root, 6, xv)
        rows_out(root, 7, xv, rt, 0, lambda i, d: d)
        finish_rows(7, 0)

    def answer(u):
        tag = tgr[u][None]
        block = jnp.where(tag == 0, zb[0], 0.0)
        for s in range(1, 2 * root_rb):
            block = jnp.where(tag == s, zb[s], block)
        return block

    def send_answer(i):
        u = (f + i) % fronts
        rk[u] = answer(u)
        remote(rk.at[u], ak.at[f], x_s.at[2], x_r.at[2], (u, b))
    loop(fronts, send_answer, 1)
    ak[f] = answer(f)
    wait_bytes(ak.at[pl.ds(0, fronts - 1)], x_r.at[2])

    def need(s):
        put(xn, s, ak[own[s]].reshape(directions, LANES))
    loop(sends, need)

    cols_out(child, 2, xn, gt, 1)
    child_step(2, base=1)
    cols_out(child, 3, xn, gt, 0, send=False)
    gather(child, 2, xvc)
    rows_out(child, 1, xvc, ct, 2, lambda i, d: d)

    def last(h):
        def use(i, v):
            cout[h, :, lanes(i)] = v
            put(xc, i, v)
        return use
    rows_in(child, 1, last(1))
    cols_out(child, 3, xc, ct, 1, add=True)
    child_step(3, base=0)
    gather(child, 3, xvc)
    rows_out(child, 2, xvc, ct, 0, lambda i, d: d)
    rows_in(child, 2, last(0))

    def sent_chunks(side, phase, count):
        wait_bytes(side.term.at[phase, pl.ds(0, 2 * count)], rs_s.at[side.rs0 + phase])

    def both(condition, yes, no):
        pl.when(condition)(yes)
        pl.when(jnp.logical_not(condition))(no)

    for side, phases in ((root, len(ROOT_SOURCES)), (child, CHILD_SUMS)):
        for phase in range(phases):
            def sums(side=side, phase=phase):
                both(mine(side), lambda: sent_chunks(side, phase, side.chunks - 1),
                     lambda: sent_chunks(side, phase, side.chunks))
            if side is root:
                on(ROOT_SOURCES[phase], sums)
            else:
                sums()
    for phase, pair in enumerate(ROOT_ROWS):
        on(pair, lambda phase=phase: wait_bytes(rows_r.at[phase, pl.ds(0, blks - 1)], blk_s.at[phase]))
    for phase in range(CHILD_ROWS):
        wait_bytes(rows_c.at[phase, pl.ds(0, blks - 1)], blk_s.at[child.blk0 + phase])

    @pl.when(mine(root))
    def _():
        for phase, target in enumerate(ROOT_TARGETS):
            if target is None:
                wait_bytes(ob.at[pl.ds(0, fronts - 1), pl.ds(0, 2)], ag_s.at[phase])
            else:
                both(p == target,
                     lambda phase=phase: wait_bytes(tgr.at[pl.ds(0, 2 * (half - 1))], ag_s.at[phase]),
                     lambda phase=phase: wait_bytes(tgr.at[pl.ds(0, 2 * half)], ag_s.at[phase]))

    @pl.when(mine(child))
    def _():
        for phase in range(CHILD_SUMS):
            wait_bytes(tgr.at[pl.ds(0, 2 * (half - 1))], ag_s.at[child.ag0 + phase])
    wait_bytes(tgs.at[pl.ds(0, fronts - 1)], x_s.at[0])
    wait_bytes(ob.at[pl.ds(0, fronts - 1)], x_s.at[1])
    wait_bytes(rk.at[pl.ds(0, fronts - 1)], x_s.at[2])


def on_device(fronts, blks, root_tiles, child_tiles, child_update, extend_map, root_side, child_side):
    root, child = root_tiles[0], child_tiles[0]
    rside, cside = root_side[0], child_side[0]
    update = jnp.transpose(child_update, (1, 0, 2))
    directions = rside.shape[1]
    half = fronts // 2
    g3 = directions // 8
    root_rb, child_rb = rside.shape[2] // LANES, cside.shape[2] // LANES
    root_cols, child_cols = root.shape[2], child.shape[2]
    root_tiles8, child_tiles8 = root_cols // LANES * g3, child_cols // LANES * g3
    sends = extend_map.shape[0]
    f32, bf16 = jnp.float32, jnp.bfloat16
    vmem, sem = pltpu.VMEM, pltpu.SemaphoreType.DMA
    sums, rows, casts = len(ROOT_SOURCES), len(ROOT_ROWS), len(ROOT_TARGETS)
    whole = pl.BlockSpec(memory_space=pltpu.VMEM)
    hbm = pl.BlockSpec(memory_space=pl.ANY)
    outs = pl.pallas_call(
        functools.partial(kernel, fronts, blks),
        out_shape=(jax.ShapeDtypeStruct(rside.shape, f32), jax.ShapeDtypeStruct(cside.shape, f32)),
        in_specs=[pl.BlockSpec(memory_space=pltpu.SMEM), whole, whole, hbm, hbm, hbm],
        out_specs=(whole, whole),
        scratch_shapes=[
            vmem(root.shape, bf16), vmem(child.shape, bf16), vmem(update.shape, bf16),
            vmem((2, root_rb, directions, LANES), f32),
            vmem((2 * directions, rside.shape[2]), bf16), vmem((2 * directions, root_cols), bf16),
            vmem((2 * directions, cside.shape[2]), bf16), vmem((2 * directions, child_cols), bf16),
            vmem((2 * directions, sends * LANES), bf16),
            vmem((sends, directions, LANES), f32),
            vmem((fronts, g3, 8, LANES), f32), vmem((fronts, g3, 8, LANES), f32),
            vmem((fronts, g3, 8, LANES), f32), vmem((fronts, g3, 8, LANES), f32),
            vmem((fronts, 8, LANES), jnp.int32), vmem((fronts, 8, LANES), jnp.int32),
            vmem((2 * root_rb, g3, 8, LANES), f32),
            vmem((rows, blks, root_rb, directions, LANES), f32), vmem((sums, root_tiles8, 8, LANES), f32),
            vmem((sums, half, 2, 8, LANES), f32), vmem((casts, root_tiles8, 8, LANES), f32),
            vmem((CHILD_ROWS, blks, child_rb, directions, LANES), f32),
            vmem((CHILD_SUMS, child_tiles8, 8, LANES), f32),
            vmem((CHILD_SUMS, half, 2, 8, LANES), f32), vmem((CHILD_SUMS, child_tiles8, 8, LANES), f32),
            pltpu.SMEM((sends,), jnp.int32), pltpu.SMEM((sends,), jnp.int32),
            pltpu.SMEM((fronts,), jnp.int32),
            sem((3 + 2 + root.shape[0],)),
            sem((rows + CHILD_ROWS,)), sem((rows + CHILD_ROWS,)),
            sem((sums + CHILD_SUMS,)), sem((sums + CHILD_SUMS,)),
            sem((casts + CHILD_SUMS,)), sem((casts + CHILD_SUMS,)),
            sem((3,)), sem((3,)),
        ],
        compiler_params=pltpu.CompilerParams(
            collective_id=0, has_side_effects=True, vmem_limit_bytes=58 * 1024 * 1024
        ),
    )(extend_map, rside, cside, root, child, update)
    return (outs[0][None], outs[1][None])


def solution(mesh):
    in_specs = (
        P("front", None, None, "blk"),
        P("front", None, None, "blk"),
        P("front", None, "blk"),
        P("front"),
        P("front", None, None, None),
        P("front", None, None, None),
    )
    out_specs = (P("front", None, None, None), P("front", None, None, None))
    body = functools.partial(on_device, mesh.shape["front"], mesh.shape["blk"])
    return jax.shard_map(body, mesh=mesh, in_specs=in_specs, out_specs=out_specs, check_vma=False)
```

```python
import functools
import types

import jax
import jax.numpy as jnp
from jax import lax
from jax.experimental import pallas as pl
from jax.experimental.pallas import tpu as pltpu
from jax.sharding import PartitionSpec as P

LANES = 128
SUB = 8
MESH = pl.DeviceIdType.MESH
ROOT_PANELS = 4

BACK_2, BACK_1, BACK_0, EARLY_1, EARLY_0 = 4, 5, 6, 7, 8
SUM_FROM = (0, 1, 1, 0, 0, 1, 1, 0, 0)
SUM_AT = (0, 1, 1, 0, 1, 1, 0, 1, 0)
CAST_FROM = (0, 1, 1, 0, 1, 1, 0)
CAST_TO = ((1, 0), (1, 0), (0,), (0,), (1,), (1,), (0,))
ROOT_ROWS = (0, 1, 1, 0, 0, 1, 1, 0)
CHILD_SUMS, CHILD_ROWS = 4, 3


def loop(count, body, start=0):
    lax.fori_loop(start, count, lambda i, c: (body(i), c)[1], 0)


def wait_bytes(ref, sem):
    pltpu.make_async_copy(ref, ref, sem).wait()


def split(value):
    high = value.astype(jnp.bfloat16).astype(jnp.float32)
    return jnp.concatenate([high, value - high], axis=0).astype(jnp.bfloat16)


def fold(product):
    return product[:SUB] + product[SUB:]


def times(x, tile):
    return jnp.dot(x, tile, preferred_element_type=jnp.float32)


def times_transposed(x, tile):
    return lax.dot_general(x, tile, (((1,), (1,)), ((), ())), preferred_element_type=jnp.float32)


def lanes(i):
    return slice(i * LANES, (i + 1) * LANES)


def aligned(index, size):
    return pl.ds(index * size if isinstance(index, int) else pl.multiple_of(index * size, size), size)


def both(condition, yes, no):
    pl.when(condition)(yes)
    pl.when(jnp.logical_not(condition))(no)


def kernel(
    fronts, blks,
    emap, rside, cside, rt_hbm, ct_hbm, gt_hbm, rout, cout,
    rt, ct, gv, gt, shuffle, run, xr, xv, xc, xvc, xn, pb, ob, ar, rk, ak, nk, tgs, tgr, zb,
    rows_r, term_r, recv_r, y_r, rows_c, term_c, recv_c, y_c,
    counts, own, place, inv,
    load_sem, blk_s, blk_r, rs_s, rs_r, ag_s, ag_r, x_s, x_r, t_s, t_r,
):
    f = lax.axis_index("front")
    b = lax.axis_index("blk")
    half = fronts // 2
    p = f // half
    q = f % half
    count_groups = rside.shape[1] // SUB
    root_rb = rside.shape[2] // LANES
    child_rb = cside.shape[2] // LANES
    sends = pb.shape[1]

    def groups(body):
        loop(count_groups, body)

    def load(src, dst, index):
        copy = pltpu.make_async_copy(src, dst, load_sem.at[index])
        copy.start()
        return copy

    loads_c = [load(ct_hbm.at[0], ct.at[0], 0)]
    load_g = load(gt_hbm, gv, 3)
    loads_c += [load(ct_hbm.at[i], ct.at[i], i) for i in (1, 2)]
    loads_r = [load(rt_hbm.at[i], rt.at[i], 4 + i) for i in range(ROOT_PANELS + 1)]

    barrier = pltpu.get_barrier_semaphore()
    loop(fronts, lambda i: pl.semaphore_signal(
        barrier, inc=1, device_id=((f + i) % fronts, b), device_id_type=MESH), 1)
    loop(blks, lambda i: pl.semaphore_signal(
        barrier, inc=1, device_id=(f, (b + i) % blks), device_id_type=MESH), 1)

    def remote(src, dst, ss, rs, device):
        pltpu.make_async_remote_copy(
            src_ref=src, dst_ref=dst, send_sem=ss, recv_sem=rs, device_id=device, device_id_type=MESH
        ).start()

    root = types.SimpleNamespace(
        rows=rows_r, term=term_r, recv=recv_r, y=y_r, blk0=0, rs0=0, ag0=0,
        per=recv_r.shape[3], chunks=term_r.shape[2] // recv_r.shape[3], rb=root_rb, x=xr, v=xv)
    child = types.SimpleNamespace(
        rows=rows_c, term=term_c, recv=recv_c, y=y_c, blk0=len(ROOT_ROWS), rs0=len(SUM_FROM),
        ag0=len(CAST_FROM), per=recv_c.shape[3], chunks=term_c.shape[2] // recv_c.shape[3], rb=child_rb,
        x=xc, v=xvc)

    def member_of(ch, g):
        return (ch + 5 * g) % half

    def chunk_of(member, g):
        return (member + half - 5 * g % half) % half

    def at_pair(side, phase, table):
        return p if side is child else table[phase]

    def mine(side, pair, g):
        holds = chunk_of(q, g) < side.chunks
        return holds if side is child else (p == pair) & holds

    def x_group(x, g):
        return x.at[aligned(g, 2 * SUB)]

    def put(x, g, i, value):
        x[aligned(g, 2 * SUB), lanes(i)] = split(value)

    def send_rows(side, phase, g):
        ref = side.rows.at[phase, g, b]
        sems = (blk_s.at[side.blk0 + phase, g], blk_r.at[side.blk0 + phase, g])
        for d in range(1, blks):
            remote(ref, ref, *sems, (f, (b + d) % blks))

    def rows_out(side, phase, g, tile, slot, base=None):
        product = fold(times_transposed(x_group(side.v, g)[...], tile[slot]))
        for i in range(side.rb):
            value = product[:, lanes(i)]
            side.rows[phase, g, b, i] = value if base is None else base(i) - value
        send_rows(side, phase, g)

    def rows_in(side, phase, g, use=None):
        wait_bytes(side.rows.at[phase, g, pl.ds(0, blks - 1)], blk_r.at[side.blk0 + phase, g])
        for i in range(side.rb):
            total = side.rows[phase, g, 0, i]
            for s in range(1, blks):
                total = total + side.rows[phase, g, s, i]
            if use is not None:
                use(i, total)
            put(side.x, g, i, total)

    def send_chunks(side, phase, g):
        pair = at_pair(side, phase, SUM_AT)
        sems = (rs_s.at[side.rs0 + phase, g], rs_r.at[side.rs0 + phase, g])

        def send(ch):
            owner = pair * half + member_of(ch, g)
            src = side.term.at[phase, g, pl.ds(side.per * ch, side.per)]

            @pl.when(owner == f)
            def _():
                side.recv[phase, g, q] = src[...]

            @pl.when(owner != f)
            def _():
                remote(src, side.recv.at[phase, g, q], *sems, (owner, b))
        loop(side.chunks, send)

    def keep_cols(side, phase, g, product, add, first=0):
        for i in range(product.shape[1] // LANES):
            value = product[:, lanes(i)]
            if add:
                value = value + side.term[phase, g, first + i]
            side.term[phase, g, first + i] = value

    def cols_out(side, phase, g, x, tile, slot, add=False):
        keep_cols(side, phase, g, fold(times(x_group(x, g)[...], tile[slot])), add)
        send_chunks(side, phase, g)

    def cols_whole(side, phase, x, tile, slot):
        width = 4 * LANES if tile.shape[2] % (4 * LANES) == 0 else LANES
        for c in range(tile.shape[2] // width):
            product = times(x[...], tile[slot, :, c * width:(c + 1) * width])
            for g in range(count_groups):
                keep_cols(side, phase, g, fold(product[2 * SUB * g:2 * SUB * (g + 1)]), False, c * width // LANES)

    def take(side, phase, g):
        sem = rs_r.at[side.rs0 + phase, g]

        def some(count):
            wait_bytes(side.recv.at[phase, g, pl.ds(0, count)], sem)
        some(half - 1 if side is child or SUM_AT[phase] == SUM_FROM[phase] else half)
        total = side.recv[phase, g, 0]
        for s in range(1, half):
            total = total + side.recv[phase, g, s]
        return total

    def spread(side, phase, g, value):
        at = pl.ds(side.per * chunk_of(q, g), side.per)
        ref = side.y.at[phase, g, at]
        side.y[phase, g, at] = value
        sems = (ag_s.at[side.ag0 + phase, g], ag_r.at[side.ag0 + phase, g])
        source = at_pair(side, phase, CAST_FROM)
        target = p if side is child else CAST_TO[phase][0]

        def send(i):
            remote(ref, ref, *sems, (target * half + (q + i) % half, b))
        loop(half, send, 1 if side is child or target == source else 0)

    def spread_more(phase, g):
        @pl.when(mine(root, CAST_FROM[phase], g))
        def _():
            ref = root.y.at[phase, g, pl.ds(root.per * chunk_of(q, g), root.per)]
            target = CAST_TO[phase][1]

            def send(i):
                remote(ref, ref, ag_s.at[phase, g], ag_r.at[phase, g], (target * half + (q + i) % half, b))
            loop(half, send, 1 if target == CAST_FROM[phase] else 0)

    def gather(side, phase, g):
        def some(count):
            wait_bytes(side.y.at[phase, g, pl.ds(0, side.per * count)], ag_r.at[side.ag0 + phase, g])
        both(mine(side, at_pair(side, phase, CAST_FROM), g), lambda: some(side.chunks - 1),
             lambda: some(side.chunks))
        for i in range(side.term.shape[2]):
            put(side.v, g, i, side.y[phase, g, i])

    def step(side, phase, out, g, base=None, early=None):
        @pl.when(mine(side, at_pair(side, phase, SUM_AT), g))
        def _():
            total = take(side, phase, g)
            if early is not None:
                total = total + take(side, early, g)
            if base is not None:
                total = side.y[base, g, pl.ds(side.per * chunk_of(q, g), side.per)] - total
            spread(side, out, g, total)

    lead = (b == 0).astype(jnp.float32)

    def side_rows(ref, h, g, i):
        return ref[h, aligned(g, SUB), lanes(i)]

    def put_child(g):
        for i in range(child_rb):
            put(xc, g, i, side_rows(cside, 0, g, i))
    groups(put_child)

    panel_blocks = half * root_rb

    def route(s):
        r = emap[s]
        k = lax.div(r, panel_blocks)
        within = lax.rem(r, panel_blocks)
        low = jnp.minimum(k, ROOT_PANELS - 1 - k)
        own[s] = half * low + lax.div(within, root_rb)
        place[s] = jnp.where(k == low, 0, root_rb) + lax.rem(within, root_rb)

    def invert(u):
        index = jnp.int32(0)
        tag = jnp.int32(-1)
        for s in range(sends):
            match = own[s] == u
            index = jnp.where(match, s, index)
            tag = jnp.where(match, place[s], tag)
        inv[u] = index
        tgs[u] = jnp.full((SUB, LANES), tag, jnp.int32)

    part_rows = 16
    slots = shuffle.shape[0]
    parts = gv.shape[0] // (part_rows * slots)

    def part(n):
        for s in range(slots):
            at = pl.ds(pl.multiple_of((n * slots + s) * part_rows, part_rows), part_rows)
            rows = gv[at].reshape(2 * part_rows, gv.shape[2]).astype(jnp.float32)
            for j in range(gv.shape[2] // LANES):
                shuffle[s, j] = rows[:, lanes(j)]
            for j in range(gv.shape[2] // LANES):
                for k in range(2):
                    gt[k, at, lanes(j)] = shuffle[s, j, pl.ds(k, part_rows, stride=2), :].astype(gt.dtype)

    loads_c[0].wait()
    cols_whole(child, 0, xc, ct, 0)
    loop(sends, route)
    loop(fronts, invert)
    pl.semaphore_wait(barrier, fronts - 1 + blks - 1)
    groups(lambda g: send_chunks(child, 0, g))
    tgr[f] = tgs[f]

    def send_tag(i):
        u = (f + i) % fronts
        remote(tgs.at[u], tgr.at[f], t_s.at[0], t_r.at[0], (u, b))
    loop(fronts, send_tag, 1)
    load_g.wait()
    loop(parts // 2, part)
    groups(lambda g: step(child, 0, 0, g))
    loop(parts, part, parts // 2)
    loads_c[1].wait()
    loads_c[2].wait()

    def child_1(g):
        gather(child, 0, g)
        rows_out(child, 0, g, ct, 1, lambda i: lead * side_rows(cside, 1, g, i))
    groups(child_1)

    def update_0():
        for s in range(0, sends, 2):
            product = times_transposed(xvc[...], gt[0, s * LANES:(s + 2) * LANES])
            for g in range(count_groups):
                rows = fold(product[2 * SUB * g:2 * SUB * (g + 1)])
                for j in range(2):
                    pb[g, s + j] = rows[:, lanes(j)]
    update_0()

    def child_2(g):
        rows_in(child, 0, g)
        cols_out(child, 1, g, xc, ct, 2)
    groups(child_2)
    groups(lambda g: step(child, 1, 1, g))

    def update_1(g):
        gather(child, 1, g)
        for s in range(0, sends, 2):
            rows = fold(times_transposed(x_group(xvc, g)[...], gt[1, s * LANES:(s + 2) * LANES]))
            for j in range(2):
                pb[g, s + j] = pb[g, s + j] + rows[:, lanes(j)]
        ar[g, f] = pb[g, inv[f]]

        def send_block(i):
            u = (f + i) % fronts
            ob[g, u] = pb[g, inv[u]]
            remote(ob.at[g, u], ar.at[g, f], x_s.at[0, g], x_r.at[0, g], (u, b))
        loop(fronts, send_block, 1)
    groups(update_1)
    for l in loads_r:
        l.wait()
    wait_bytes(tgr.at[pl.ds(0, fronts - 1)], t_r.at[0])

    def land(g):
        wait_bytes(ar.at[g, pl.ds(0, fronts - 1)], x_r.at[0, g])

        def add(u, totals):
            block = ar[g, u]
            tag = tgr[u]
            return tuple(t + jnp.where(tag == s, block, 0.0) for s, t in enumerate(totals))
        zero = jnp.zeros((SUB, LANES), jnp.float32)
        landed = lax.fori_loop(0, fronts, add, (zero,) * (2 * root_rb), unroll=4)
        for h in range(2):
            for i in range(root_rb):
                run[g, h, i] = lead * side_rows(rside, h, g, i) - landed[h * root_rb + i]

    def on(pair, body):
        pl.when(p == pair)(body)

    def subtract(slot):
        width = 2 * LANES
        for c in range(0, root_rb * LANES, width):
            size = min(width, root_rb * LANES - c)
            product = times_transposed(xv[...], rt[slot, c:c + size])
            for g in range(count_groups):
                rows = fold(product[2 * SUB * g:2 * SUB * (g + 1)])
                for j in range(size // LANES):
                    run[g, 1, c // LANES + j] = run[g, 1, c // LANES + j] - rows[:, lanes(j)]

    def solve(phase, slot):
        def one(g):
            rows_in(root, phase, g)
            cols_out(root, phase, g, xr, rt, slot)
        groups(one)

    def advance(cast, phase, h, slot):
        def one(g):
            gather(root, cast, g)
            rows_out(root, phase, g, rt, slot, lambda i: run[g, h, i])
        groups(one)

    def retreat(cast, phase, h, slot):
        def one(g):
            gather(root, cast, g)
            rows_out(root, phase, g, rt, slot)
        groups(one)

    def finish(phase, h, after):
        def one(g):
            def use(i, v):
                zb[g, h * root_rb + i] = v
                rout[h, aligned(g, SUB), lanes(i)] = v
            rows_in(root, phase, g, use)
            after(g)
        groups(one)

    def answers(g):
        def answer(u):
            tag = tgr[u]
            block = jnp.where(tag == 0, zb[g, 0], 0.0)
            for s in range(1, 2 * root_rb):
                block = jnp.where(tag == s, zb[g, s], block)
            return block

        def send_answer(i):
            u = (f + i) % fronts
            rk[g, u] = answer(u)
            remote(rk.at[g, u], ak.at[g, f], x_s.at[1, g], x_r.at[1, g], (u, b))
        loop(fronts, send_answer, 1)
        ak[g, f] = answer(f)

    def first(g):
        land(g)

        @pl.when(p == 0)
        def _():
            for i in range(root_rb):
                rows_r[0, g, b, i] = run[g, 0, i]
            send_rows(root, 0, g)
    groups(first)

    @functools.partial(on, 0)
    def _():
        solve(0, 0)
        groups(lambda g: step(root, 0, 0, g))
        groups(lambda g: spread_more(0, g))
        groups(lambda g: gather(root, 0, g))
        subtract(1)
        groups(lambda g: gather(root, 1, g))
        subtract(2)
        advance(2, 3, 1, 3)
        solve(3, 4)
        groups(lambda g: step(root, 3, 3, g))
        retreat(3, 4, 1, 4)
        finish(4, 1, lambda g: cols_out(root, BACK_2, g, xr, rt, 3))
        cols_whole(root, EARLY_1, xr, rt, 2)
        groups(lambda g: send_chunks(root, EARLY_1, g))
        cols_whole(root, EARLY_0, xr, rt, 1)
        groups(lambda g: send_chunks(root, EARLY_0, g))
        groups(lambda g: step(root, BACK_0, 6, g, base=0, early=EARLY_0))
        retreat(6, 7, 0, 0)
        finish(7, 0, lambda g: answers(g))

    @functools.partial(on, 1)
    def _():
        advance(0, 1, 0, 0)
        subtract(2)
        solve(1, 1)
        groups(lambda g: step(root, 1, 1, g))
        advance(1, 2, 1, 3)
        groups(lambda g: spread_more(1, g))
        solve(2, 4)
        groups(lambda g: step(root, 2, 2, g))
        groups(lambda g: step(root, BACK_2, 4, g, base=2))
        retreat(4, 5, 1, 4)
        finish(5, 1, lambda g: cols_out(root, BACK_1, g, xr, rt, 3))
        cols_whole(root, BACK_0, xr, rt, 2)
        groups(lambda g: step(root, BACK_1, 5, g, base=1, early=EARLY_1))
        retreat(5, 6, 0, 1)
        finish(6, 0, lambda g: cols_out(root, BACK_0, g, xr, rt, 0, add=True))
        groups(lambda g: answers(g))

    def child_3(g):
        wait_bytes(ak.at[g, pl.ds(0, fronts - 1)], x_r.at[1, g])

        def keep(u):
            nk[u] = ak[g, u]
        loop(fronts, keep)
        for s in range(sends):
            put(xn, g, s, nk[own[s]])
        cols_out(child, 2, g, xn, gt, 1)
    groups(child_3)
    cols_whole(child, 3, xn, gt, 0)
    groups(lambda g: step(child, 2, 2, g, base=1))

    def child_4(g):
        gather(child, 2, g)
        rows_out(child, 1, g, ct, 2)
    groups(child_4)

    def last(h, g):
        def use(i, v):
            cout[h, aligned(g, SUB), lanes(i)] = v
        return use

    def child_5(g):
        rows_in(child, 1, g, last(1, g))
        cols_out(child, 3, g, xc, ct, 1, add=True)
    groups(child_5)
    groups(lambda g: step(child, 3, 3, g, base=0))

    def child_6(g):
        gather(child, 3, g)
        rows_out(child, 2, g, ct, 0)
    groups(child_6)
    groups(lambda g: rows_in(child, 2, g, last(0, g)))

    def drain(g):
        def sent_chunks(side, phase, count):
            wait_bytes(side.term.at[phase, g, pl.ds(0, side.per * count)], rs_s.at[side.rs0 + phase, g])

        def sent_terms(side, phase, same):
            if same:
                both(mine(side, at_pair(side, phase, SUM_AT), g),
                     lambda: sent_chunks(side, phase, side.chunks - 1),
                     lambda: sent_chunks(side, phase, side.chunks))
            else:
                sent_chunks(side, phase, side.chunks)
        for phase in range(len(SUM_FROM)):
            on(SUM_FROM[phase], lambda phase=phase: sent_terms(root, phase, SUM_FROM[phase] == SUM_AT[phase]))
        for phase in range(CHILD_SUMS):
            sent_terms(child, phase, True)
        for phase, pair in enumerate(ROOT_ROWS):
            on(pair, lambda phase=phase: wait_bytes(rows_r.at[phase, g, pl.ds(0, blks - 1)], blk_s.at[phase, g]))
        for phase in range(CHILD_ROWS):
            wait_bytes(rows_c.at[phase, g, pl.ds(0, blks - 1)], blk_s.at[child.blk0 + phase, g])
        for phase, source in enumerate(CAST_FROM):
            @pl.when(mine(root, source, g))
            def _(phase=phase, source=source):
                count = half * len(CAST_TO[phase]) - (source in CAST_TO[phase])
                wait_bytes(counts.at[pl.ds(0, count)], ag_s.at[phase, g])

        @pl.when(mine(child, None, g))
        def _():
            for phase in range(CHILD_SUMS):
                wait_bytes(recv_c.at[phase, g, pl.ds(0, half - 1)], ag_s.at[child.ag0 + phase, g])
        wait_bytes(ob.at[g, pl.ds(0, fronts - 1)], x_s.at[0, g])
        wait_bytes(rk.at[g, pl.ds(0, fronts - 1)], x_s.at[1, g])
    groups(drain)
    wait_bytes(tgs.at[pl.ds(0, fronts - 1)], t_s.at[0])


def on_device(fronts, blks, root_tiles, child_tiles, child_update, extend_map, root_side, child_side):
    root, child = root_tiles[0], child_tiles[0]
    rside, cside = root_side[0], child_side[0]
    directions = rside.shape[1]
    groups = directions // SUB
    half = fronts // 2
    root_rb, child_rb = rside.shape[2] // LANES, cside.shape[2] // LANES
    root_cols, child_cols = root.shape[2], child.shape[2]
    root_blocks, child_blocks = root_cols // LANES, child_cols // LANES
    update_rows, panels, _ = child_update.shape
    sends = extend_map.shape[0]
    root_per = -(-root_blocks // half)
    child_per = -(-child_blocks // half)
    f32, bf16 = jnp.float32, jnp.bfloat16
    vmem, sem = pltpu.VMEM, pltpu.SemaphoreType.DMA
    sums, rows, casts = len(SUM_FROM), len(ROOT_ROWS), len(CAST_FROM)
    whole = pl.BlockSpec(memory_space=pltpu.VMEM)
    hbm = pl.BlockSpec(memory_space=pl.ANY)
    tile = (SUB, LANES)
    outs = pl.pallas_call(
        functools.partial(kernel, fronts, blks),
        out_shape=(jax.ShapeDtypeStruct(rside.shape, f32), jax.ShapeDtypeStruct(cside.shape, f32)),
        in_specs=[pl.BlockSpec(memory_space=pltpu.SMEM), whole, whole, hbm, hbm, hbm],
        out_specs=(whole, whole),
        scratch_shapes=[
            vmem(root.shape, bf16), vmem(child.shape, bf16), vmem(child_update.shape, bf16),
            vmem((panels, update_rows, child_cols), bf16), vmem((4, child_blocks, 32, LANES), f32),
            vmem((groups, 2, root_rb) + tile, f32),
            vmem((2 * directions, rside.shape[2]), bf16), vmem((2 * directions, root_cols), bf16),
            vmem((2 * directions, cside.shape[2]), bf16), vmem((2 * directions, child_cols), bf16),
            vmem((2 * directions, sends * LANES), bf16),
            vmem((groups, sends) + tile, f32),
            vmem((groups, fronts) + tile, f32), vmem((groups, fronts) + tile, f32),
            vmem((groups, fronts) + tile, f32), vmem((groups, fronts) + tile, f32),
            vmem((fronts,) + tile, f32),
            vmem((fronts,) + tile, jnp.int32), vmem((fronts,) + tile, jnp.int32),
            vmem((groups, 2 * root_rb) + tile, f32),
            vmem((rows, groups, blks, root_rb) + tile, f32), vmem((sums, groups, root_blocks) + tile, f32),
            vmem((sums, groups, half, root_per) + tile, f32), vmem((casts, groups, root_blocks) + tile, f32),
            vmem((CHILD_ROWS, groups, blks, child_rb) + tile, f32),
            vmem((CHILD_SUMS, groups, child_blocks) + tile, f32),
            vmem((CHILD_SUMS, groups, half, child_per) + tile, f32),
            vmem((CHILD_SUMS, groups, child_blocks) + tile, f32),
            vmem((fronts, root_per) + tile, f32),
            pltpu.SMEM((sends,), jnp.int32), pltpu.SMEM((sends,), jnp.int32),
            pltpu.SMEM((fronts,), jnp.int32),
            sem((4 + root.shape[0],)),
            sem((rows + CHILD_ROWS, groups)), sem((rows + CHILD_ROWS, groups)),
            sem((sums + CHILD_SUMS, groups)), sem((sums + CHILD_SUMS, groups)),
            sem((casts + CHILD_SUMS, groups)), sem((casts + CHILD_SUMS, groups)),
            sem((2, groups)), sem((2, groups)), sem((1,)), sem((1,)),
        ],
        compiler_params=pltpu.CompilerParams(
            collective_id=0, has_side_effects=True, vmem_limit_bytes=58 * 1024 * 1024
        ),
    )(extend_map, rside, cside, root, child, child_update)
    return (outs[0][None], outs[1][None])


def solution(mesh):
    in_specs = (
        P("front", None, None, "blk"),
        P("front", None, None, "blk"),
        P("front", None, "blk"),
        P("front"),
        P("front", None, None, None),
        P("front", None, None, None),
    )
    out_specs = (P("front", None, None, None), P("front", None, None, None))
    body = functools.partial(on_device, mesh.shape["front"], mesh.shape["blk"])
    return jax.shard_map(body, mesh=mesh, in_specs=in_specs, out_specs=out_specs, check_vma=False)
```

```python
import functools
import types

import jax
import jax.numpy as jnp
from jax import lax
from jax.experimental import pallas as pl
from jax.experimental.pallas import tpu as pltpu
from jax.sharding import PartitionSpec as P

LANES = 128
SUB = 8
MESH = pl.DeviceIdType.MESH
ROOT_PANELS = 4

BACK_2, BACK_1, BACK_0, EARLY_1, EARLY_0 = 4, 5, 6, 7, 8
SUM_FROM = (0, 1, 1, 0, 0, 1, 1, 0, 0)
SUM_AT = (0, 1, 1, 0, 1, 1, 0, 1, 0)
CAST_FROM = (0, 1, 1, 0, 1, 1, 0)
CAST_TO = ((1, 0), (1, 0), (0,), (0,), (1,), (1,), (0,))
ROOT_ROWS = (0, 1, 1, 0, 0, 1, 1, 0)
CHILD_SUMS, CHILD_ROWS = 4, 3


def loop(count, body, start=0):
    lax.fori_loop(start, count, lambda i, c: (body(i), c)[1], 0)


def wait_bytes(ref, sem):
    pltpu.make_async_copy(ref, ref, sem).wait()


def split(value):
    high = value.astype(jnp.bfloat16).astype(jnp.float32)
    return jnp.concatenate([high, value - high], axis=0).astype(jnp.bfloat16)


def fold(product):
    return product[:SUB] + product[SUB:]


def times(x, tile):
    return jnp.dot(x, tile, preferred_element_type=jnp.float32)


def times_transposed(x, tile):
    return lax.dot_general(x, tile, (((1,), (1,)), ((), ())), preferred_element_type=jnp.float32)


def lanes(i):
    return slice(i * LANES, (i + 1) * LANES)


def aligned(index, size):
    return pl.ds(index * size if isinstance(index, int) else pl.multiple_of(index * size, size), size)


def both(condition, yes, no):
    pl.when(condition)(yes)
    pl.when(jnp.logical_not(condition))(no)


def kernel(
    fronts, blks,
    emap, rside, cside, rt_hbm, ct_hbm, gt_hbm, rout, cout,
    rt, ct, gv, gt, shuffle, run, xr, xv, xc, xvc, xn, pb, ob, ar, rk, ak, nk, tgs, tgr, zb,
    rows_r, term_r, recv_r, y_r, rows_c, term_c, recv_c, y_c,
    counts, own, place, inv,
    load_sem, blk_s, blk_r, rs_s, rs_r, ag_s, ag_r, x_s, x_r, t_s, t_r, free,
):
    f = lax.axis_index("front")
    b = lax.axis_index("blk")
    half = fronts // 2
    p = lax.div(f, half)
    q = lax.rem(f, half)
    count_groups = rside.shape[1] // SUB
    root_rb = rside.shape[2] // LANES
    child_rb = cside.shape[2] // LANES
    sends = pb.shape[1]

    def groups(body):
        loop(count_groups, body)

    def load(src, dst, index):
        copy = pltpu.make_async_copy(src, dst, load_sem.at[index])
        copy.start()
        return copy

    loads_c = [load(ct_hbm.at[0], ct.at[0], 0)]
    load_g = load(gt_hbm, gv, 3)
    loads_c += [load(ct_hbm.at[i], ct.at[i], i) for i in (1, 2)]
    loads_r = [load(rt_hbm.at[i], rt.at[i], 4 + i) for i in range(ROOT_PANELS + 1)]

    barrier = pltpu.get_barrier_semaphore()
    loop(fronts, lambda i: pl.semaphore_signal(
        barrier, inc=1, device_id=(lax.rem(f + i, fronts), b), device_id_type=MESH), 1)
    loop(blks, lambda i: pl.semaphore_signal(
        barrier, inc=1, device_id=(f, lax.rem(b + i, blks)), device_id_type=MESH), 1)

    def remote(src, dst, ss, rs, device):
        pltpu.make_async_remote_copy(
            src_ref=src, dst_ref=dst, send_sem=ss, recv_sem=rs, device_id=device, device_id_type=MESH
        ).start()

    root = types.SimpleNamespace(
        rows=rows_r, term=term_r, recv=recv_r, y=y_r, blk0=0, rs0=0, ag0=0,
        per=recv_r.shape[3], chunks=term_r.shape[2] // recv_r.shape[3], rb=root_rb, x=xr, v=xv)
    child = types.SimpleNamespace(
        rows=rows_c, term=term_c, recv=recv_c, y=y_c, blk0=len(ROOT_ROWS), rs0=len(SUM_FROM),
        ag0=len(CAST_FROM), per=recv_c.shape[3], chunks=term_c.shape[2] // recv_c.shape[3], rb=child_rb,
        x=xc, v=xvc)

    def member_of(ch, g):
        return lax.rem(ch + 5 * g, half)

    def chunk_of(member, g):
        return lax.rem(member + 4 * half - 5 * g, half)

    def at_pair(side, phase, table):
        return p if side is child else table[phase]

    def mine(side, pair, g):
        holds = chunk_of(q, g) < side.chunks
        return holds if side is child else (p == pair) & holds

    def x_group(x, g):
        return x.at[aligned(g, 2 * SUB)]

    def put(x, g, i, value):
        x[aligned(g, 2 * SUB), lanes(i)] = split(value)

    def send_rows(side, phase, g):
        ref = side.rows.at[phase, g, b]
        sems = (blk_s.at[side.blk0 + phase, g], blk_r.at[side.blk0 + phase, g])
        for d in range(1, blks):
            remote(ref, ref, *sems, (f, lax.rem(b + d, blks)))

    def rows_out(side, phase, g, tile, slot, base=None):
        product = fold(times_transposed(x_group(side.v, g)[...], tile[slot]))
        for i in range(side.rb):
            value = product[:, lanes(i)]
            side.rows[phase, g, b, i] = value if base is None else base(i) - value
        send_rows(side, phase, g)

    def rows_in(side, phase, g, use=None):
        wait_bytes(side.rows.at[phase, g, pl.ds(0, blks - 1)], blk_r.at[side.blk0 + phase, g])
        for i in range(side.rb):
            total = side.rows[phase, g, 0, i]
            for s in range(1, blks):
                total = total + side.rows[phase, g, s, i]
            if use is not None:
                use(i, total)
            put(side.x, g, i, total)

    def send_chunks(side, phase, g):
        pair = at_pair(side, phase, SUM_AT)
        sems = (rs_s.at[side.rs0 + phase, g], rs_r.at[side.rs0 + phase, g])

        def send(ch):
            owner = pair * half + member_of(ch, g)
            src = side.term.at[phase, g, pl.ds(side.per * ch, side.per)]

            @pl.when(owner == f)
            def _():
                side.recv[phase, g, q] = src[...]

            @pl.when(owner != f)
            def _():
                remote(src, side.recv.at[phase, g, q], *sems, (owner, b))
        loop(side.chunks, send)

    def keep_cols(side, phase, g, product, add, first=0):
        for i in range(product.shape[1] // LANES):
            value = product[:, lanes(i)]
            if add:
                value = value + side.term[phase, g, first + i]
            side.term[phase, g, first + i] = value

    def cols_out(side, phase, g, x, tile, slot, add=False):
        keep_cols(side, phase, g, fold(times(x_group(x, g)[...], tile[slot])), add)
        send_chunks(side, phase, g)

    def cols_whole(side, phase, x, tile, slot):
        width = 4 * LANES if tile.shape[2] % (4 * LANES) == 0 else LANES
        for c in range(tile.shape[2] // width):
            product = times(x[...], tile[slot, :, c * width:(c + 1) * width])
            for g in range(count_groups):
                keep_cols(side, phase, g, fold(product[2 * SUB * g:2 * SUB * (g + 1)]), False, c * width // LANES)

    def take(side, phase, g):
        sem = rs_r.at[side.rs0 + phase, g]

        def some(count):
            wait_bytes(side.recv.at[phase, g, pl.ds(0, count)], sem)
        some(half - 1 if side is child or SUM_AT[phase] == SUM_FROM[phase] else half)
        total = side.recv[phase, g, 0]
        for s in range(1, half):
            total = total + side.recv[phase, g, s]
        return total

    def spread(side, phase, g, value):
        at = pl.ds(side.per * chunk_of(q, g), side.per)
        ref = side.y.at[phase, g, at]
        side.y[phase, g, at] = value
        sems = (ag_s.at[side.ag0 + phase, g], ag_r.at[side.ag0 + phase, g])
        source = at_pair(side, phase, CAST_FROM)
        target = p if side is child else CAST_TO[phase][0]

        def send(i):
            remote(ref, ref, *sems, (target * half + lax.rem(q + i, half), b))
        loop(half, send, 1 if side is child or target == source else 0)

    def spread_more(phase, g):
        @pl.when(mine(root, CAST_FROM[phase], g))
        def _():
            ref = root.y.at[phase, g, pl.ds(root.per * chunk_of(q, g), root.per)]
            target = CAST_TO[phase][1]

            def send(i):
                remote(ref, ref, ag_s.at[phase, g], ag_r.at[phase, g], (target * half + lax.rem(q + i, half), b))
            loop(half, send, 1 if target == CAST_FROM[phase] else 0)

    def gather(side, phase, g):
        def some(count):
            wait_bytes(side.y.at[phase, g, pl.ds(0, side.per * count)], ag_r.at[side.ag0 + phase, g])
        both(mine(side, at_pair(side, phase, CAST_FROM), g), lambda: some(side.chunks - 1),
             lambda: some(side.chunks))
        for i in range(side.term.shape[2]):
            put(side.v, g, i, side.y[phase, g, i])

    def step(side, phase, out, g, base=None, early=None):
        @pl.when(mine(side, at_pair(side, phase, SUM_AT), g))
        def _():
            total = take(side, phase, g)
            if early is not None:
                total = total + take(side, early, g)
            if base is not None:
                total = side.y[base, g, pl.ds(side.per * chunk_of(q, g), side.per)] - total
            spread(side, out, g, total)

    lead = (b == 0).astype(jnp.float32)

    def side_rows(ref, h, g, i):
        return ref[h, aligned(g, SUB), lanes(i)]

    def put_child(g):
        for i in range(child_rb):
            put(xc, g, i, side_rows(cside, 0, g, i))
    groups(put_child)

    panel_blocks = half * root_rb

    def route(s):
        r = emap[s]
        k = lax.div(r, panel_blocks)
        within = lax.rem(r, panel_blocks)
        low = jnp.minimum(k, ROOT_PANELS - 1 - k)
        own[s] = half * low + lax.div(within, root_rb)
        place[s] = jnp.where(k == low, 0, root_rb) + lax.rem(within, root_rb)

    def invert(u):
        index = jnp.int32(0)
        tag = jnp.int32(-1)
        for s in range(sends):
            match = own[s] == u
            index = jnp.where(match, s, index)
            tag = jnp.where(match, place[s], tag)
        inv[u] = index
        tgs[u] = jnp.full((SUB, LANES), tag, jnp.int32)

    part_rows = 16
    slots = shuffle.shape[0]
    parts = gv.shape[0] // (part_rows * slots)

    def part(n):
        for s in range(slots):
            at = pl.ds(pl.multiple_of((n * slots + s) * part_rows, part_rows), part_rows)
            rows = gv[at].reshape(2 * part_rows, gv.shape[2]).astype(jnp.float32)
            for j in range(gv.shape[2] // LANES):
                shuffle[s, j] = rows[:, lanes(j)]
            for j in range(gv.shape[2] // LANES):
                for k in range(2):
                    gt[k, at, lanes(j)] = shuffle[s, j, pl.ds(k, part_rows, stride=2), :].astype(gt.dtype)

    loads_c[0].wait()
    cols_whole(child, 0, xc, ct, 0)
    loop(sends, route)
    loop(fronts, invert)
    pl.semaphore_wait(barrier, fronts - 1 + blks - 1)
    groups(lambda g: send_chunks(child, 0, g))
    tgr[f] = tgs[f]

    def send_tag(i):
        u = lax.rem(f + i, fronts)
        remote(tgs.at[u], tgr.at[f], t_s.at[0], t_r.at[0], (u, b))
    loop(fronts, send_tag, 1)
    load_g.wait()
    loop(parts // 2, part)
    groups(lambda g: step(child, 0, 0, g))
    loop(parts, part, parts // 2)
    loads_c[1].wait()
    loads_c[2].wait()

    def child_1(g):
        gather(child, 0, g)
        rows_out(child, 0, g, ct, 1, lambda i: lead * side_rows(cside, 1, g, i))
    groups(child_1)

    def update_0():
        for s in range(0, sends, 2):
            product = times_transposed(xvc[...], gt[0, s * LANES:(s + 2) * LANES])
            for g in range(count_groups):
                rows = fold(product[2 * SUB * g:2 * SUB * (g + 1)])
                for j in range(2):
                    pb[g, s + j] = rows[:, lanes(j)]
    update_0()

    def child_2(g):
        rows_in(child, 0, g)
        cols_out(child, 1, g, xc, ct, 2)
    groups(child_2)
    groups(lambda g: step(child, 1, 1, g))

    def update_1(g):
        gather(child, 1, g)
        for s in range(0, sends, 2):
            rows = fold(times_transposed(x_group(xvc, g)[...], gt[1, s * LANES:(s + 2) * LANES]))
            for j in range(2):
                pb[g, s + j] = pb[g, s + j] + rows[:, lanes(j)]
        ar[g, f] = pb[g, inv[f]]

        def send_block(i):
            u = lax.rem(f + i, fronts)
            ob[g, u] = pb[g, inv[u]]
            remote(ob.at[g, u], ar.at[g, f], x_s.at[0, g], x_r.at[0, g], (u, b))
        loop(fronts, send_block, 1)
    groups(update_1)
    for l in loads_r:
        l.wait()
    wait_bytes(tgr.at[pl.ds(0, fronts - 1)], t_r.at[0])

    def land(g):
        wait_bytes(ar.at[g, pl.ds(0, fronts - 1)], x_r.at[0, g])

        def add(u, totals):
            block = ar[g, u]
            tag = tgr[u]
            return tuple(t + jnp.where(tag == s, block, 0.0) for s, t in enumerate(totals))
        zero = jnp.zeros((SUB, LANES), jnp.float32)
        landed = lax.fori_loop(0, fronts, add, (zero,) * (2 * root_rb), unroll=4)
        for h in range(2):
            for i in range(root_rb):
                run[g, h, i] = lead * side_rows(rside, h, g, i) - landed[h * root_rb + i]

    def on(pair, body):
        pl.when(p == pair)(body)

    def subtract(slot):
        width = 2 * LANES
        for c in range(0, root_rb * LANES, width):
            size = min(width, root_rb * LANES - c)
            product = times_transposed(xv[...], rt[slot, c:c + size])
            for g in range(count_groups):
                rows = fold(product[2 * SUB * g:2 * SUB * (g + 1)])
                for j in range(size // LANES):
                    run[g, 1, c // LANES + j] = run[g, 1, c // LANES + j] - rows[:, lanes(j)]

    def solve(phase, slot):
        def one(g):
            rows_in(root, phase, g)
            cols_out(root, phase, g, xr, rt, slot)
        groups(one)

    def advance(cast, phase, h, slot):
        def one(g):
            gather(root, cast, g)
            rows_out(root, phase, g, rt, slot, lambda i: run[g, h, i])
        groups(one)

    def retreat(cast, phase, h, slot):
        def one(g):
            gather(root, cast, g)
            rows_out(root, phase, g, rt, slot)
        groups(one)

    def finish(phase, h, after):
        def one(g):
            def use(i, v):
                zb[g, h * root_rb + i] = v
                rout[h, aligned(g, SUB), lanes(i)] = v
            rows_in(root, phase, g, use)
            after(g)
        groups(one)

    def answers(g):
        def answer(u):
            tag = tgr[u]
            block = jnp.where(tag == 0, zb[g, 0], 0.0)
            for s in range(1, 2 * root_rb):
                block = jnp.where(tag == s, zb[g, s], block)
            return block

        def send_answer(i):
            u = lax.rem(f + i, fronts)
            rk[g, u] = answer(u)
            remote(rk.at[g, u], ak.at[g, f], x_s.at[1, g], x_r.at[1, g], (u, b))
        loop(fronts, send_answer, 1)
        ak[g, f] = answer(f)

    def first(g):
        land(g)

        @pl.when(p == 0)
        def _():
            for i in range(root_rb):
                rows_r[0, g, b, i] = run[g, 0, i]
            send_rows(root, 0, g)
    groups(first)

    def links_free(index):
        pl.semaphore_signal(free.at[index], inc=1, device_id=(f - half, b), device_id_type=MESH)

    @functools.partial(on, 0)
    def _():
        solve(0, 0)
        groups(lambda g: step(root, 0, 0, g))
        pl.semaphore_wait(free.at[0], 1)
        groups(lambda g: spread_more(0, g))
        groups(lambda g: gather(root, 0, g))
        subtract(1)
        groups(lambda g: gather(root, 1, g))
        subtract(2)
        advance(2, 3, 1, 3)
        solve(3, 4)
        groups(lambda g: step(root, 3, 3, g))
        retreat(3, 4, 1, 4)
        finish(4, 1, lambda g: cols_out(root, BACK_2, g, xr, rt, 3))
        cols_whole(root, EARLY_1, xr, rt, 2)
        cols_whole(root, EARLY_0, xr, rt, 1)
        pl.semaphore_wait(free.at[1], 1)
        groups(lambda g: send_chunks(root, EARLY_1, g))
        groups(lambda g: send_chunks(root, EARLY_0, g))
        groups(lambda g: step(root, BACK_0, 6, g, base=0, early=EARLY_0))
        retreat(6, 7, 0, 0)
        finish(7, 0, lambda g: answers(g))

    @functools.partial(on, 1)
    def _():
        advance(0, 1, 0, 0)
        links_free(0)
        subtract(2)
        solve(1, 1)
        groups(lambda g: step(root, 1, 1, g))
        advance(1, 2, 1, 3)
        groups(lambda g: spread_more(1, g))
        solve(2, 4)
        groups(lambda g: step(root, 2, 2, g))
        groups(lambda g: step(root, BACK_2, 4, g, base=2))
        retreat(4, 5, 1, 4)
        links_free(1)
        finish(5, 1, lambda g: cols_out(root, BACK_1, g, xr, rt, 3))
        cols_whole(root, BACK_0, xr, rt, 2)
        groups(lambda g: step(root, BACK_1, 5, g, base=1, early=EARLY_1))
        retreat(5, 6, 0, 1)
        finish(6, 0, lambda g: cols_out(root, BACK_0, g, xr, rt, 0, add=True))
        groups(lambda g: answers(g))

    def drain_terms(side, phase, g, same):
        def some(count):
            wait_bytes(side.term.at[phase, g, pl.ds(0, side.per * count)], rs_s.at[side.rs0 + phase, g])
        if same:
            both(mine(side, at_pair(side, phase, SUM_AT), g), lambda: some(side.chunks - 1), lambda: some(side.chunks))
        else:
            some(side.chunks)

    def drain_rows(side, phase, g):
        wait_bytes(side.rows.at[phase, g, pl.ds(0, blks - 1)], blk_s.at[side.blk0 + phase, g])

    def drain_root(g):
        for pair in range(2):
            @functools.partial(on, pair)
            def _(pair=pair):
                for phase, source in enumerate(SUM_FROM):
                    if source == pair:
                        drain_terms(root, phase, g, SUM_AT[phase] == pair)
                for phase, source in enumerate(ROOT_ROWS):
                    if source == pair:
                        drain_rows(root, phase, g)

                @pl.when(mine(root, pair, g))
                def _():
                    for phase, source in enumerate(CAST_FROM):
                        if source == pair:
                            count = half * len(CAST_TO[phase]) - (source in CAST_TO[phase])
                            wait_bytes(counts.at[pl.ds(0, count)], ag_s.at[phase, g])

    def drain_child(g, sums, rows):
        for phase in sums:
            drain_terms(child, phase, g, True)
        for phase in rows:
            drain_rows(child, phase, g)

        @pl.when(mine(child, None, g))
        def _():
            for phase in sums:
                wait_bytes(recv_c.at[phase, g, pl.ds(0, half - 1)], ag_s.at[child.ag0 + phase, g])

    def child_3(g):
        wait_bytes(ak.at[g, pl.ds(0, fronts - 1)], x_r.at[1, g])

        def keep(u):
            nk[u] = ak[g, u]
        loop(fronts, keep)
        for s in range(sends):
            put(xn, g, s, nk[own[s]])
        cols_out(child, 2, g, xn, gt, 1)
    groups(child_3)
    cols_whole(child, 3, xn, gt, 0)
    groups(drain_root)
    groups(lambda g: step(child, 2, 2, g, base=1))

    def child_4(g):
        gather(child, 2, g)
        rows_out(child, 1, g, ct, 2)
    groups(child_4)

    def last(h, g):
        def use(i, v):
            cout[h, aligned(g, SUB), lanes(i)] = v
        return use

    def child_5(g):
        rows_in(child, 1, g, last(1, g))
        cols_out(child, 3, g, xc, ct, 1, add=True)
    groups(child_5)

    def drain_early(g):
        drain_child(g, (0, 1), (0, 1))
        wait_bytes(ob.at[g, pl.ds(0, fronts - 1)], x_s.at[0, g])
        wait_bytes(rk.at[g, pl.ds(0, fronts - 1)], x_s.at[1, g])
    groups(drain_early)
    wait_bytes(tgs.at[pl.ds(0, fronts - 1)], t_s.at[0])
    groups(lambda g: step(child, 3, 3, g, base=0))
    groups(lambda g: drain_child(g, (2,), ()))

    def child_6(g):
        gather(child, 3, g)
        rows_out(child, 2, g, ct, 0)
    groups(child_6)
    groups(lambda g: rows_in(child, 2, g, last(0, g)))

    groups(lambda g: drain_child(g, (3,), (2,)))

def place_fields(root_in, child_in, root_out, child_out):
    root_out[0] = root_in[...]
    child_out[0] = child_in[...]


def on_device(fronts, blks, root_tiles, child_tiles, child_update, extend_map, root_side, child_side):
    root, child = root_tiles[0], child_tiles[0]
    rside, cside = root_side[0], child_side[0]
    directions = rside.shape[1]
    groups = directions // SUB
    half = fronts // 2
    root_rb, child_rb = rside.shape[2] // LANES, cside.shape[2] // LANES
    root_cols, child_cols = root.shape[2], child.shape[2]
    root_blocks, child_blocks = root_cols // LANES, child_cols // LANES
    update_rows, panels, _ = child_update.shape
    sends = extend_map.shape[0]
    root_per = -(-root_blocks // half)
    child_per = -(-child_blocks // half)
    f32, bf16 = jnp.float32, jnp.bfloat16
    vmem, sem = pltpu.VMEM, pltpu.SemaphoreType.DMA
    sums, rows, casts = len(SUM_FROM), len(ROOT_ROWS), len(CAST_FROM)
    whole = pl.BlockSpec(memory_space=pltpu.VMEM)
    hbm = pl.BlockSpec(memory_space=pl.ANY)
    tile = (SUB, LANES)
    outs = pl.pallas_call(
        functools.partial(kernel, fronts, blks),
        out_shape=(jax.ShapeDtypeStruct(rside.shape, f32), jax.ShapeDtypeStruct(cside.shape, f32)),
        in_specs=[pl.BlockSpec(memory_space=pltpu.SMEM), whole, whole, hbm, hbm, hbm],
        out_specs=(whole, whole),
        scratch_shapes=[
            vmem(root.shape, bf16), vmem(child.shape, bf16), vmem(child_update.shape, bf16),
            vmem((panels, update_rows, child_cols), bf16), vmem((4, child_blocks, 32, LANES), f32),
            vmem((groups, 2, root_rb) + tile, f32),
            vmem((2 * directions, rside.shape[2]), bf16), vmem((2 * directions, root_cols), bf16),
            vmem((2 * directions, cside.shape[2]), bf16), vmem((2 * directions, child_cols), bf16),
            vmem((2 * directions, sends * LANES), bf16),
            vmem((groups, sends) + tile, f32),
            vmem((groups, fronts) + tile, f32), vmem((groups, fronts) + tile, f32),
            vmem((groups, fronts) + tile, f32), vmem((groups, fronts) + tile, f32),
            vmem((fronts,) + tile, f32),
            vmem((fronts,) + tile, jnp.int32), vmem((fronts,) + tile, jnp.int32),
            vmem((groups, 2 * root_rb) + tile, f32),
            vmem((rows, groups, blks, root_rb) + tile, f32), vmem((sums, groups, root_blocks) + tile, f32),
            vmem((sums, groups, half, root_per) + tile, f32), vmem((casts, groups, root_blocks) + tile, f32),
            vmem((CHILD_ROWS, groups, blks, child_rb) + tile, f32),
            vmem((CHILD_SUMS, groups, child_blocks) + tile, f32),
            vmem((CHILD_SUMS, groups, half, child_per) + tile, f32),
            vmem((CHILD_SUMS, groups, child_blocks) + tile, f32),
            vmem((fronts, root_per) + tile, f32),
            pltpu.SMEM((sends,), jnp.int32), pltpu.SMEM((sends,), jnp.int32),
            pltpu.SMEM((fronts,), jnp.int32),
            sem((4 + root.shape[0],)),
            sem((rows + CHILD_ROWS, groups)), sem((rows + CHILD_ROWS, groups)),
            sem((sums + CHILD_SUMS, groups)), sem((sums + CHILD_SUMS, groups)),
            sem((casts + CHILD_SUMS, groups)), sem((casts + CHILD_SUMS, groups)),
            sem((2, groups)), sem((2, groups)), sem((1,)), sem((1,)),
            pltpu.SemaphoreType.REGULAR((2,)),
        ],
        compiler_params=pltpu.CompilerParams(
            collective_id=0, has_side_effects=True, vmem_limit_bytes=58 * 1024 * 1024
        ),
    )(extend_map, rside, cside, root, child, child_update)
    outs = pl.pallas_call(
        place_fields,
        out_shape=tuple(jax.ShapeDtypeStruct((1,) + o.shape, f32) for o in outs),
        in_specs=[whole, whole], out_specs=(whole, whole),
    )(*outs)
    return tuple(outs)


def solution(mesh):
    in_specs = (
        P("front", None, None, "blk"),
        P("front", None, None, "blk"),
        P("front", None, "blk"),
        P("front"),
        P("front", None, None, None),
        P("front", None, None, None),
    )
    out_specs = (P("front", None, None, None), P("front", None, None, None))
    body = functools.partial(on_device, mesh.shape["front"], mesh.shape["blk"])
    return jax.shard_map(body, mesh=mesh, in_specs=in_specs, out_specs=out_specs, check_vma=False)
```

```python
import functools
import types

import jax
import jax.numpy as jnp
from jax import lax
from jax.experimental import pallas as pl
from jax.experimental.pallas import tpu as pltpu
from jax.sharding import PartitionSpec as P

LANES = 128
SUB = 8
MESH = pl.DeviceIdType.MESH
ROOT_PANELS = 4

BACK_2, BACK_1, BACK_0, EARLY_1, EARLY_0 = 4, 5, 6, 7, 8
SUM_FROM = (0, 1, 1, 0, 0, 1, 1, 0, 0)
SUM_AT = (0, 1, 1, 0, 1, 1, 0, 0, 0)
CAST_FROM = (0, 1, 1, 0, 1, 1, 0, 0)
CAST_TO = ((1, 0), (1,), (0,), (0,), (1,), (1,), (0,), (0,))
AGAIN_1 = 7
ROOT_ROWS = (0, 1, 1, 0, 0, 1, 1, 0)
CHILD_SUMS, CHILD_ROWS = 4, 3


def loop(count, body, start=0):
    lax.fori_loop(start, count, lambda i, c: (body(i), c)[1], 0)


def wait_bytes(ref, sem):
    pltpu.make_async_copy(ref, ref, sem).wait()


def split(value):
    high = value.astype(jnp.bfloat16).astype(jnp.float32)
    return jnp.concatenate([high, value - high], axis=0).astype(jnp.bfloat16)


def fold(product):
    return product[:SUB] + product[SUB:]


def times(x, tile):
    return jnp.dot(x, tile, preferred_element_type=jnp.float32)


def times_transposed(x, tile):
    return lax.dot_general(x, tile, (((1,), (1,)), ((), ())), preferred_element_type=jnp.float32)


def lanes(i):
    return slice(i * LANES, (i + 1) * LANES)


def aligned(index, size):
    return pl.ds(index * size if isinstance(index, int) else pl.multiple_of(index * size, size), size)


def both(condition, yes, no):
    pl.when(condition)(yes)
    pl.when(jnp.logical_not(condition))(no)


def kernel(
    fronts, blks,
    emap, rside, cside, rt_hbm, ct_hbm, gt_hbm, rout, cout,
    rt, ct, gv, gt, shuffle, run, xr, xv, xc, xvc, xn, pb, ob, ar, rk, ak, nk, tgs, tgr, zb,
    rows_r, term_r, recv_r, y_r, rows_c, term_c, recv_c, y_c,
    counts, relay_in, relay_out, own, place, inv,
    load_sem, blk_s, blk_r, rs_s, rs_r, ag_s, ag_r, x_s, x_r, t_s, t_r, relay_s, relay_r, free,
):
    f = lax.axis_index("front")
    b = lax.axis_index("blk")
    half = fronts // 2
    p = lax.div(f, half)
    q = lax.rem(f, half)
    count_groups = rside.shape[1] // SUB
    root_rb = rside.shape[2] // LANES
    child_rb = cside.shape[2] // LANES
    sends = pb.shape[1]

    def groups(body):
        loop(count_groups, body)

    def load(src, dst, index):
        copy = pltpu.make_async_copy(src, dst, load_sem.at[index])
        copy.start()
        return copy

    loads_c = [load(ct_hbm.at[0], ct.at[0], 0)]
    load_g = load(gt_hbm, gv, 3)
    loads_c += [load(ct_hbm.at[i], ct.at[i], i) for i in (1, 2)]
    loads_r = [load(rt_hbm.at[i], rt.at[i], 4 + i) for i in range(ROOT_PANELS + 1)]

    barrier = pltpu.get_barrier_semaphore()
    loop(fronts, lambda i: pl.semaphore_signal(
        barrier, inc=1, device_id=(lax.rem(f + i, fronts), b), device_id_type=MESH), 1)
    loop(blks, lambda i: pl.semaphore_signal(
        barrier, inc=1, device_id=(f, lax.rem(b + i, blks)), device_id_type=MESH), 1)

    def remote(src, dst, ss, rs, device):
        pltpu.make_async_remote_copy(
            src_ref=src, dst_ref=dst, send_sem=ss, recv_sem=rs, device_id=device, device_id_type=MESH
        ).start()

    root = types.SimpleNamespace(
        rows=rows_r, term=term_r, recv=recv_r, y=y_r, blk0=0, rs0=0, ag0=0,
        per=recv_r.shape[3], chunks=term_r.shape[2] // recv_r.shape[3], rb=root_rb, x=xr, v=xv)
    child = types.SimpleNamespace(
        rows=rows_c, term=term_c, recv=recv_c, y=y_c, blk0=len(ROOT_ROWS), rs0=len(SUM_FROM),
        ag0=len(CAST_FROM), per=recv_c.shape[3], chunks=term_c.shape[2] // recv_c.shape[3], rb=child_rb,
        x=xc, v=xvc)

    def member_of(ch, g):
        return lax.rem(ch + 5 * g, half)

    def chunk_of(member, g):
        return lax.rem(member + 4 * half - 5 * g, half)

    def at_pair(side, phase, table):
        return p if side is child else table[phase]

    def mine(side, pair, g):
        holds = chunk_of(q, g) < side.chunks
        return holds if side is child else (p == pair) & holds

    def x_group(x, g):
        return x.at[aligned(g, 2 * SUB)]

    def put(x, g, i, value):
        x[aligned(g, 2 * SUB), lanes(i)] = split(value)

    def send_rows(side, phase, g):
        ref = side.rows.at[phase, g, b]
        sems = (blk_s.at[side.blk0 + phase, g], blk_r.at[side.blk0 + phase, g])
        for d in range(1, blks):
            remote(ref, ref, *sems, (f, lax.rem(b + d, blks)))

    def rows_out(side, phase, g, tile, slot, base=None):
        product = fold(times_transposed(x_group(side.v, g)[...], tile[slot]))
        for i in range(side.rb):
            value = product[:, lanes(i)]
            side.rows[phase, g, b, i] = value if base is None else base(i) - value
        send_rows(side, phase, g)

    def rows_in(side, phase, g, use=None):
        wait_bytes(side.rows.at[phase, g, pl.ds(0, blks - 1)], blk_r.at[side.blk0 + phase, g])
        for i in range(side.rb):
            total = side.rows[phase, g, 0, i]
            for s in range(1, blks):
                total = total + side.rows[phase, g, s, i]
            if use is not None:
                use(i, total)
            put(side.x, g, i, total)

    def send_chunks(side, phase, g):
        pair = at_pair(side, phase, SUM_AT)
        sems = (rs_s.at[side.rs0 + phase, g], rs_r.at[side.rs0 + phase, g])

        def send(ch):
            owner = pair * half + member_of(ch, g)
            src = side.term.at[phase, g, pl.ds(side.per * ch, side.per)]

            @pl.when(owner == f)
            def _():
                side.recv[phase, g, q] = src[...]

            @pl.when(owner != f)
            def _():
                remote(src, side.recv.at[phase, g, q], *sems, (owner, b))
        loop(side.chunks, send)

    def keep_cols(side, phase, g, product, add, first=0):
        for i in range(product.shape[1] // LANES):
            value = product[:, lanes(i)]
            if add:
                value = value + side.term[phase, g, first + i]
            side.term[phase, g, first + i] = value

    def cols_out(side, phase, g, x, tile, slot, add=False):
        keep_cols(side, phase, g, fold(times(x_group(x, g)[...], tile[slot])), add)
        send_chunks(side, phase, g)

    def cols_whole(side, phase, x, tile, slot):
        width = 4 * LANES if tile.shape[2] % (4 * LANES) == 0 else LANES
        for c in range(tile.shape[2] // width):
            product = times(x[...], tile[slot, :, c * width:(c + 1) * width])
            for g in range(count_groups):
                keep_cols(side, phase, g, fold(product[2 * SUB * g:2 * SUB * (g + 1)]), False, c * width // LANES)

    def take(side, phase, g):
        sem = rs_r.at[side.rs0 + phase, g]

        def some(count):
            wait_bytes(side.recv.at[phase, g, pl.ds(0, count)], sem)
        some(half - 1 if side is child or SUM_AT[phase] == SUM_FROM[phase] else half)
        total = side.recv[phase, g, 0]
        for s in range(1, half):
            total = total + side.recv[phase, g, s]
        return total

    def spread(side, phase, g, value):
        at = pl.ds(side.per * chunk_of(q, g), side.per)
        ref = side.y.at[phase, g, at]
        side.y[phase, g, at] = value
        sems = (ag_s.at[side.ag0 + phase, g], ag_r.at[side.ag0 + phase, g])
        source = at_pair(side, phase, CAST_FROM)
        target = p if side is child else CAST_TO[phase][0]

        def send(i):
            remote(ref, ref, *sems, (target * half + lax.rem(q + i, half), b))
        loop(half, send, 1 if side is child or target == source else 0)

    def spread_more(phase, g):
        @pl.when(mine(root, CAST_FROM[phase], g))
        def _():
            ref = root.y.at[phase, g, pl.ds(root.per * chunk_of(q, g), root.per)]
            target = CAST_TO[phase][1]

            def send(i):
                remote(ref, ref, ag_s.at[phase, g], ag_r.at[phase, g], (target * half + lax.rem(q + i, half), b))
            loop(half, send, 1 if target == CAST_FROM[phase] else 0)

    def gather(side, phase, g):
        def some(count):
            wait_bytes(side.y.at[phase, g, pl.ds(0, side.per * count)], ag_r.at[side.ag0 + phase, g])
        both(mine(side, at_pair(side, phase, CAST_FROM), g), lambda: some(side.chunks - 1),
             lambda: some(side.chunks))
        for i in range(side.term.shape[2]):
            put(side.v, g, i, side.y[phase, g, i])

    def step(side, phase, out, g, base=None, early=None):
        @pl.when(mine(side, at_pair(side, phase, SUM_AT), g))
        def _():
            total = take(side, phase, g)
            if early is not None:
                total = total + early(g)
            if base is not None:
                total = side.y[base, g, pl.ds(side.per * chunk_of(q, g), side.per)] - total
            spread(side, out, g, total)

    lead = (b == 0).astype(jnp.float32)

    def side_rows(ref, h, g, i):
        return ref[h, aligned(g, SUB), lanes(i)]

    def put_child(g):
        for i in range(child_rb):
            put(xc, g, i, side_rows(cside, 0, g, i))
    groups(put_child)

    panel_blocks = half * root_rb

    def route(s):
        r = emap[s]
        k = lax.div(r, panel_blocks)
        within = lax.rem(r, panel_blocks)
        low = jnp.minimum(k, ROOT_PANELS - 1 - k)
        own[s] = half * low + lax.div(within, root_rb)
        place[s] = jnp.where(k == low, 0, root_rb) + lax.rem(within, root_rb)

    def invert(u):
        index = jnp.int32(0)
        tag = jnp.int32(-1)
        for s in range(sends):
            match = own[s] == u
            index = jnp.where(match, s, index)
            tag = jnp.where(match, place[s], tag)
        inv[u] = index
        tgs[u] = jnp.full((SUB, LANES), tag, jnp.int32)

    part_rows = 16
    slots = shuffle.shape[0]
    parts = gv.shape[0] // (part_rows * slots)

    def part(n):
        for s in range(slots):
            at = pl.ds(pl.multiple_of((n * slots + s) * part_rows, part_rows), part_rows)
            rows = gv[at].reshape(2 * part_rows, gv.shape[2]).astype(jnp.float32)
            for j in range(gv.shape[2] // LANES):
                shuffle[s, j] = rows[:, lanes(j)]
            for j in range(gv.shape[2] // LANES):
                for k in range(2):
                    gt[k, at, lanes(j)] = shuffle[s, j, pl.ds(k, part_rows, stride=2), :].astype(gt.dtype)

    loads_c[0].wait()
    cols_whole(child, 0, xc, ct, 0)
    loop(sends, route)
    loop(fronts, invert)
    pl.semaphore_wait(barrier, fronts - 1 + blks - 1)
    groups(lambda g: send_chunks(child, 0, g))
    tgr[f] = tgs[f]

    def send_tag(i):
        u = lax.rem(f + i, fronts)
        remote(tgs.at[u], tgr.at[f], t_s.at[0], t_r.at[0], (u, b))
    loop(fronts, send_tag, 1)
    load_g.wait()
    loop(parts // 2, part)
    groups(lambda g: step(child, 0, 0, g))
    loop(parts, part, parts // 2)
    loads_c[1].wait()
    loads_c[2].wait()

    def child_1(g):
        gather(child, 0, g)
        rows_out(child, 0, g, ct, 1, lambda i: lead * side_rows(cside, 1, g, i))
    groups(child_1)

    def update_0():
        for s in range(0, sends, 2):
            product = times_transposed(xvc[...], gt[0, s * LANES:(s + 2) * LANES])
            for g in range(count_groups):
                rows = fold(product[2 * SUB * g:2 * SUB * (g + 1)])
                for j in range(2):
                    pb[g, s + j] = rows[:, lanes(j)]
    update_0()

    def child_2(g):
        rows_in(child, 0, g)
        cols_out(child, 1, g, xc, ct, 2)
    groups(child_2)
    groups(lambda g: step(child, 1, 1, g))

    def update_1(g):
        gather(child, 1, g)
        for s in range(0, sends, 2):
            rows = fold(times_transposed(x_group(xvc, g)[...], gt[1, s * LANES:(s + 2) * LANES]))
            for j in range(2):
                pb[g, s + j] = pb[g, s + j] + rows[:, lanes(j)]
        ar[g, f] = pb[g, inv[f]]

        def send_block(i):
            u = lax.rem(f + i, fronts)
            ob[g, u] = pb[g, inv[u]]
            remote(ob.at[g, u], ar.at[g, f], x_s.at[0, g], x_r.at[0, g], (u, b))
        loop(fronts, send_block, 1)
    groups(update_1)
    for l in loads_r:
        l.wait()
    wait_bytes(tgr.at[pl.ds(0, fronts - 1)], t_r.at[0])

    def land(g):
        wait_bytes(ar.at[g, pl.ds(0, fronts - 1)], x_r.at[0, g])

        def add(u, totals):
            block = ar[g, u]
            tag = tgr[u]
            return tuple(t + jnp.where(tag == s, block, 0.0) for s, t in enumerate(totals))
        zero = jnp.zeros((SUB, LANES), jnp.float32)
        landed = lax.fori_loop(0, fronts, add, (zero,) * (2 * root_rb), unroll=16)
        for h in range(2):
            for i in range(root_rb):
                run[g, h, i] = lead * side_rows(rside, h, g, i) - landed[h * root_rb + i]

    def on(pair, body):
        pl.when(p == pair)(body)

    def subtract(slot):
        width = 2 * LANES
        for c in range(0, root_rb * LANES, width):
            size = min(width, root_rb * LANES - c)
            product = times_transposed(xv[...], rt[slot, c:c + size])
            for g in range(count_groups):
                rows = fold(product[2 * SUB * g:2 * SUB * (g + 1)])
                for j in range(size // LANES):
                    run[g, 1, c // LANES + j] = run[g, 1, c // LANES + j] - rows[:, lanes(j)]

    def solve(phase, slot):
        def one(g):
            rows_in(root, phase, g)
            cols_out(root, phase, g, xr, rt, slot)
        groups(one)

    def advance(cast, phase, h, slot):
        def one(g):
            gather(root, cast, g)
            rows_out(root, phase, g, rt, slot, lambda i: run[g, h, i])
        groups(one)

    def retreat(cast, phase, h, slot):
        def one(g):
            gather(root, cast, g)
            rows_out(root, phase, g, rt, slot)
        groups(one)

    def finish(phase, h, after):
        def one(g):
            def use(i, v):
                zb[g, h * root_rb + i] = v
                rout[h, aligned(g, SUB), lanes(i)] = v
            rows_in(root, phase, g, use)
            after(g)
        groups(one)

    def answers(g):
        def answer(u):
            tag = tgr[u]
            block = jnp.where(tag == 0, zb[g, 0], 0.0)
            for s in range(1, 2 * root_rb):
                block = jnp.where(tag == s, zb[g, s], block)
            return block

        def send_answer(i):
            u = lax.rem(f + i, fronts)
            rk[g, u] = answer(u)
            remote(rk.at[g, u], ak.at[g, f], x_s.at[1, g], x_r.at[1, g], (u, b))
        loop(fronts, send_answer, 1)
        ak[g, f] = answer(f)

    def first(g):
        land(g)

        @pl.when(p == 0)
        def _():
            for i in range(root_rb):
                rows_r[0, g, b, i] = run[g, 0, i]
            send_rows(root, 0, g)
    groups(first)

    def relay(index, g, value, peer):
        relay_out[index, g] = value
        remote(relay_out.at[index, g], relay_in.at[index, g], relay_s.at[index, g], relay_r.at[index, g], (peer, b))

    def relayed(index, g):
        wait_bytes(relay_in.at[index, g], relay_r.at[index, g])
        return relay_in[index, g]

    def relay_y(g):
        @pl.when(mine(root, 1, g))
        def _():
            relay(0, g, root.y[1, g, pl.ds(root.per * chunk_of(q, g), root.per)], f - half)

    def spread_y(g):
        @pl.when(mine(root, 0, g))
        def _():
            spread(root, AGAIN_1, g, relayed(0, g))

    def relay_sum(g):
        @pl.when(mine(root, 0, g))
        def _():
            relay(1, g, take(root, EARLY_1, g), f + half)

    def links_free(index):
        pl.semaphore_signal(free.at[index], inc=1, device_id=(f - half, b), device_id_type=MESH)

    @functools.partial(on, 0)
    def _():
        solve(0, 0)
        groups(lambda g: step(root, 0, 0, g))
        pl.semaphore_wait(free.at[0], 1)
        groups(lambda g: spread_more(0, g))
        groups(lambda g: gather(root, 0, g))
        subtract(1)
        groups(spread_y)
        groups(lambda g: gather(root, AGAIN_1, g))
        subtract(2)
        advance(2, 3, 1, 3)
        solve(3, 4)
        groups(lambda g: step(root, 3, 3, g))
        retreat(3, 4, 1, 4)
        finish(4, 1, lambda g: cols_out(root, BACK_2, g, xr, rt, 3))
        cols_whole(root, EARLY_1, xr, rt, 2)
        cols_whole(root, EARLY_0, xr, rt, 1)
        pl.semaphore_wait(free.at[1], 1)
        groups(lambda g: send_chunks(root, EARLY_1, g))
        groups(lambda g: send_chunks(root, EARLY_0, g))
        groups(relay_sum)
        groups(lambda g: step(root, BACK_0, 6, g, base=0, early=lambda g: take(root, EARLY_0, g)))
        retreat(6, 7, 0, 0)
        finish(7, 0, lambda g: answers(g))

    @functools.partial(on, 1)
    def _():
        advance(0, 1, 0, 0)
        links_free(0)
        subtract(2)
        solve(1, 1)
        groups(lambda g: step(root, 1, 1, g))
        advance(1, 2, 1, 3)
        groups(relay_y)
        solve(2, 4)
        groups(lambda g: step(root, 2, 2, g))
        groups(lambda g: step(root, BACK_2, 4, g, base=2))
        links_free(1)
        retreat(4, 5, 1, 4)
        finish(5, 1, lambda g: cols_out(root, BACK_1, g, xr, rt, 3))
        cols_whole(root, BACK_0, xr, rt, 2)
        groups(lambda g: step(root, BACK_1, 5, g, base=1, early=lambda g: relayed(1, g)))
        retreat(5, 6, 0, 1)
        finish(6, 0, lambda g: cols_out(root, BACK_0, g, xr, rt, 0, add=True))
        groups(lambda g: answers(g))

    def drain_terms(side, phase, g, same):
        def some(count):
            wait_bytes(side.term.at[phase, g, pl.ds(0, side.per * count)], rs_s.at[side.rs0 + phase, g])
        if same:
            both(mine(side, at_pair(side, phase, SUM_AT), g), lambda: some(side.chunks - 1), lambda: some(side.chunks))
        else:
            some(side.chunks)

    def drain_rows(side, phase, g):
        wait_bytes(side.rows.at[phase, g, pl.ds(0, blks - 1)], blk_s.at[side.blk0 + phase, g])

    def drain_root(g):
        for pair in range(2):
            @functools.partial(on, pair)
            def _(pair=pair):
                for phase, source in enumerate(SUM_FROM):
                    if source == pair:
                        drain_terms(root, phase, g, SUM_AT[phase] == pair)
                for phase, source in enumerate(ROOT_ROWS):
                    if source == pair:
                        drain_rows(root, phase, g)

                @pl.when(mine(root, pair, g))
                def _():
                    wait_bytes(relay_out.at[1 - pair, g], relay_s.at[1 - pair, g])
                    for phase, source in enumerate(CAST_FROM):
                        if source == pair:
                            count = half * len(CAST_TO[phase]) - (source in CAST_TO[phase])
                            wait_bytes(counts.at[pl.ds(0, count)], ag_s.at[phase, g])

    def drain_child(g, sums, rows):
        for phase in sums:
            drain_terms(child, phase, g, True)
        for phase in rows:
            drain_rows(child, phase, g)

        @pl.when(mine(child, None, g))
        def _():
            for phase in sums:
                wait_bytes(recv_c.at[phase, g, pl.ds(0, half - 1)], ag_s.at[child.ag0 + phase, g])

    def child_3(g):
        wait_bytes(ak.at[g, pl.ds(0, fronts - 1)], x_r.at[1, g])

        def keep(u):
            nk[u] = ak[g, u]
        loop(fronts, keep)
        for s in range(sends):
            put(xn, g, s, nk[own[s]])
        cols_out(child, 2, g, xn, gt, 1)
    groups(child_3)
    cols_whole(child, 3, xn, gt, 0)
    groups(drain_root)
    groups(lambda g: step(child, 2, 2, g, base=1))

    def child_4(g):
        gather(child, 2, g)
        rows_out(child, 1, g, ct, 2)
    groups(child_4)

    def last(h, g):
        def use(i, v):
            cout[h, aligned(g, SUB), lanes(i)] = v
        return use

    def child_5(g):
        rows_in(child, 1, g, last(1, g))
        cols_out(child, 3, g, xc, ct, 1, add=True)
    groups(child_5)

    def drain_early(g):
        drain_child(g, (0, 1), (0, 1))
        wait_bytes(ob.at[g, pl.ds(0, fronts - 1)], x_s.at[0, g])
        wait_bytes(rk.at[g, pl.ds(0, fronts - 1)], x_s.at[1, g])
    groups(drain_early)
    wait_bytes(tgs.at[pl.ds(0, fronts - 1)], t_s.at[0])
    groups(lambda g: step(child, 3, 3, g, base=0))
    groups(lambda g: drain_child(g, (2,), ()))

    def child_6(g):
        gather(child, 3, g)
        rows_out(child, 2, g, ct, 0)
    groups(child_6)
    groups(lambda g: rows_in(child, 2, g, last(0, g)))

    groups(lambda g: drain_child(g, (3,), (2,)))

def place_fields(root_in, child_in, root_out, child_out):
    root_out[0] = root_in[...]
    child_out[0] = child_in[...]


def on_device(fronts, blks, root_tiles, child_tiles, child_update, extend_map, root_side, child_side):
    root, child = root_tiles[0], child_tiles[0]
    rside, cside = root_side[0], child_side[0]
    directions = rside.shape[1]
    groups = directions // SUB
    half = fronts // 2
    root_rb, child_rb = rside.shape[2] // LANES, cside.shape[2] // LANES
    root_cols, child_cols = root.shape[2], child.shape[2]
    root_blocks, child_blocks = root_cols // LANES, child_cols // LANES
    update_rows, panels, _ = child_update.shape
    sends = extend_map.shape[0]
    root_per = -(-root_blocks // half)
    child_per = -(-child_blocks // half)
    f32, bf16 = jnp.float32, jnp.bfloat16
    vmem, sem = pltpu.VMEM, pltpu.SemaphoreType.DMA
    sums, rows, casts = len(SUM_FROM), len(ROOT_ROWS), len(CAST_FROM)
    whole = pl.BlockSpec(memory_space=pltpu.VMEM)
    hbm = pl.BlockSpec(memory_space=pl.ANY)
    tile = (SUB, LANES)
    outs = pl.pallas_call(
        functools.partial(kernel, fronts, blks),
        out_shape=(jax.ShapeDtypeStruct(rside.shape, f32), jax.ShapeDtypeStruct(cside.shape, f32)),
        in_specs=[pl.BlockSpec(memory_space=pltpu.SMEM), whole, whole, hbm, hbm, hbm],
        out_specs=(whole, whole),
        scratch_shapes=[
            vmem(root.shape, bf16), vmem(child.shape, bf16), vmem(child_update.shape, bf16),
            vmem((panels, update_rows, child_cols), bf16), vmem((4, child_blocks, 32, LANES), f32),
            vmem((groups, 2, root_rb) + tile, f32),
            vmem((2 * directions, rside.shape[2]), bf16), vmem((2 * directions, root_cols), bf16),
            vmem((2 * directions, cside.shape[2]), bf16), vmem((2 * directions, child_cols), bf16),
            vmem((2 * directions, sends * LANES), bf16),
            vmem((groups, sends) + tile, f32),
            vmem((groups, fronts) + tile, f32), vmem((groups, fronts) + tile, f32),
            vmem((groups, fronts) + tile, f32), vmem((groups, fronts) + tile, f32),
            vmem((fronts,) + tile, f32),
            vmem((fronts,) + tile, jnp.int32), vmem((fronts,) + tile, jnp.int32),
            vmem((groups, 2 * root_rb) + tile, f32),
            vmem((rows, groups, blks, root_rb) + tile, f32), vmem((sums, groups, root_blocks) + tile, f32),
            vmem((sums, groups, half, root_per) + tile, f32), vmem((casts, groups, root_blocks) + tile, f32),
            vmem((CHILD_ROWS, groups, blks, child_rb) + tile, f32),
            vmem((CHILD_SUMS, groups, child_blocks) + tile, f32),
            vmem((CHILD_SUMS, groups, half, child_per) + tile, f32),
            vmem((CHILD_SUMS, groups, child_blocks) + tile, f32),
            vmem((fronts, root_per) + tile, f32),
            vmem((2, groups, root_per) + tile, f32), vmem((2, groups, root_per) + tile, f32),
            pltpu.SMEM((sends,), jnp.int32), pltpu.SMEM((sends,), jnp.int32),
            pltpu.SMEM((fronts,), jnp.int32),
            sem((4 + root.shape[0],)),
            sem((rows + CHILD_ROWS, groups)), sem((rows + CHILD_ROWS, groups)),
            sem((sums + CHILD_SUMS, groups)), sem((sums + CHILD_SUMS, groups)),
            sem((casts + CHILD_SUMS, groups)), sem((casts + CHILD_SUMS, groups)),
            sem((2, groups)), sem((2, groups)), sem((1,)), sem((1,)),
            sem((2, groups)), sem((2, groups)),
            pltpu.SemaphoreType.REGULAR((2,)),
        ],
        compiler_params=pltpu.CompilerParams(
            collective_id=0, has_side_effects=True, vmem_limit_bytes=58 * 1024 * 1024
        ),
    )(extend_map, rside, cside, root, child, child_update)
    outs = pl.pallas_call(
        place_fields,
        out_shape=tuple(jax.ShapeDtypeStruct((1,) + o.shape, f32) for o in outs),
        in_specs=[whole, whole], out_specs=(whole, whole),
    )(*outs)
    return tuple(outs)


def solution(mesh):
    in_specs = (
        P("front", None, None, "blk"),
        P("front", None, None, "blk"),
        P("front", None, "blk"),
        P("front"),
        P("front", None, None, None),
        P("front", None, None, None),
    )
    out_specs = (P("front", None, None, None), P("front", None, None, None))
    body = functools.partial(on_device, mesh.shape["front"], mesh.shape["blk"])
    return jax.shard_map(body, mesh=mesh, in_specs=in_specs, out_specs=out_specs, check_vma=False)
```

```python
import functools
import types

import jax
import jax.numpy as jnp
from jax import lax
from jax.experimental import pallas as pl
from jax.experimental.pallas import tpu as pltpu
from jax.sharding import PartitionSpec as P

LANES = 128
SUB = 8
MESH = pl.DeviceIdType.MESH
ROOT_PANELS = 4

BACK_2, BACK_1, BACK_0, EARLY_1, EARLY_0 = 4, 5, 6, 7, 8
SUM_FROM = (0, 1, 1, 0, 0, 1, 1, 0, 0)
SUM_AT = (0, 1, 1, 0, 1, 1, 0, 0, 0)
CAST_FROM = (0, 1, 1, 0, 1, 1, 0, 0)
CAST_TO = ((1, 0), (1,), (0,), (0,), (1,), (1,), (0,), (0,))
AGAIN_1 = 7
ROOT_ROWS = (0, 1, 1, 0, 0, 1, 1, 0)
CHILD_SUMS, CHILD_ROWS = 4, 3


def loop(count, body, start=0):
    lax.fori_loop(start, count, lambda i, c: (body(i), c)[1], 0)


def wait_bytes(ref, sem):
    pltpu.make_async_copy(ref, ref, sem).wait()


def split(value):
    high = value.astype(jnp.bfloat16).astype(jnp.float32)
    return jnp.concatenate([high, value - high], axis=0).astype(jnp.bfloat16)


def fold(product):
    return product[:SUB] + product[SUB:]


def times(x, tile):
    return jnp.dot(x, tile, preferred_element_type=jnp.float32)


def times_transposed(x, tile):
    return lax.dot_general(x, tile, (((1,), (1,)), ((), ())), preferred_element_type=jnp.float32)


def lanes(i):
    return slice(i * LANES, (i + 1) * LANES)


def aligned(index, size):
    return pl.ds(index * size if isinstance(index, int) else pl.multiple_of(index * size, size), size)


def both(condition, yes, no):
    pl.when(condition)(yes)
    pl.when(jnp.logical_not(condition))(no)


def kernel(
    fronts, blks,
    emap, rside, cside, rt_hbm, ct_hbm, gt_hbm, rout, cout,
    rt, ct, gv, gt, shuffle, run, xr, xv, xc, xvc, xn, pb, ob, ar, rk, ak, nk, tgs, tgr, zb,
    rows_r, term_r, recv_r, y_r, rows_c, term_c, recv_c, y_c,
    counts, relay_in, relay_out, own, place, inv,
    load_sem, blk_s, blk_r, rs_s, rs_r, ag_s, ag_r, x_s, x_r, t_s, t_r, relay_s, relay_r, free,
):
    f = lax.axis_index("front")
    b = lax.axis_index("blk")
    half = fronts // 2
    p = lax.div(f, half)
    q = lax.rem(f, half)
    count_groups = rside.shape[1] // SUB
    root_rb = rside.shape[2] // LANES
    child_rb = cside.shape[2] // LANES
    sends = pb.shape[1]

    def groups(body):
        loop(count_groups, body)

    def load(src, dst, index):
        copy = pltpu.make_async_copy(src, dst, load_sem.at[index])
        copy.start()
        return copy

    loads_c = [load(ct_hbm.at[0], ct.at[0], 0)]
    load_g = load(gt_hbm, gv, 3)
    loads_c += [load(ct_hbm.at[i], ct.at[i], i) for i in (1, 2)]
    loads_r = [load(rt_hbm.at[i], rt.at[i], 4 + i) for i in range(ROOT_PANELS + 1)]

    barrier = pltpu.get_barrier_semaphore()
    loop(fronts, lambda i: pl.semaphore_signal(
        barrier, inc=1, device_id=(lax.rem(f + i, fronts), b), device_id_type=MESH), 1)
    loop(blks, lambda i: pl.semaphore_signal(
        barrier, inc=1, device_id=(f, lax.rem(b + i, blks)), device_id_type=MESH), 1)

    def remote(src, dst, ss, rs, device):
        pltpu.make_async_remote_copy(
            src_ref=src, dst_ref=dst, send_sem=ss, recv_sem=rs, device_id=device, device_id_type=MESH
        ).start()

    root = types.SimpleNamespace(
        rows=rows_r, term=term_r, recv=recv_r, y=y_r, blk0=0, rs0=0, ag0=0,
        per=recv_r.shape[3], chunks=term_r.shape[2] // recv_r.shape[3], rb=root_rb, x=xr, v=xv)
    child = types.SimpleNamespace(
        rows=rows_c, term=term_c, recv=recv_c, y=y_c, blk0=len(ROOT_ROWS), rs0=len(SUM_FROM),
        ag0=len(CAST_FROM), per=recv_c.shape[3], chunks=term_c.shape[2] // recv_c.shape[3], rb=child_rb,
        x=xc, v=xvc)

    def member_of(ch, g):
        return lax.rem(ch + 5 * g, half)

    def chunk_of(member, g):
        return lax.rem(member + 4 * half - 5 * g, half)

    def at_pair(side, phase, table):
        return p if side is child else table[phase]

    def mine(side, pair, g):
        holds = chunk_of(q, g) < side.chunks
        return holds if side is child else (p == pair) & holds

    def x_group(x, g):
        return x.at[aligned(g, 2 * SUB)]

    def put(x, g, i, value):
        x[aligned(g, 2 * SUB), lanes(i)] = split(value)

    def send_rows(side, phase, g):
        ref = side.rows.at[phase, g, b]
        sems = (blk_s.at[side.blk0 + phase, g], blk_r.at[side.blk0 + phase, g])
        for d in range(1, blks):
            remote(ref, ref, *sems, (f, lax.rem(b + d, blks)))

    def rows_out(side, phase, g, tile, slot, base=None):
        product = fold(times_transposed(x_group(side.v, g)[...], tile[slot]))
        for i in range(side.rb):
            value = product[:, lanes(i)]
            side.rows[phase, g, b, i] = value if base is None else base(i) - value
        send_rows(side, phase, g)

    def rows_in(side, phase, g, use=None):
        wait_bytes(side.rows.at[phase, g, pl.ds(0, blks - 1)], blk_r.at[side.blk0 + phase, g])
        for i in range(side.rb):
            total = side.rows[phase, g, 0, i]
            for s in range(1, blks):
                total = total + side.rows[phase, g, s, i]
            if use is not None:
                use(i, total)
            put(side.x, g, i, total)

    def send_chunks(side, phase, g):
        pair = at_pair(side, phase, SUM_AT)
        sems = (rs_s.at[side.rs0 + phase, g], rs_r.at[side.rs0 + phase, g])

        def send(ch):
            owner = pair * half + member_of(ch, g)
            src = side.term.at[phase, g, pl.ds(side.per * ch, side.per)]

            @pl.when(owner == f)
            def _():
                side.recv[phase, g, q] = src[...]

            @pl.when(owner != f)
            def _():
                remote(src, side.recv.at[phase, g, q], *sems, (owner, b))
        loop(side.chunks, send)

    def keep_cols(side, phase, g, product, add, first=0):
        for i in range(product.shape[1] // LANES):
            value = product[:, lanes(i)]
            if add:
                value = value + side.term[phase, g, first + i]
            side.term[phase, g, first + i] = value

    def cols_out(side, phase, g, x, tile, slot, add=False):
        keep_cols(side, phase, g, fold(times(x_group(x, g)[...], tile[slot])), add)
        send_chunks(side, phase, g)

    def cols_whole(side, phase, x, tile, slot):
        width = 4 * LANES if tile.shape[2] % (4 * LANES) == 0 else LANES
        for c in range(tile.shape[2] // width):
            product = times(x[...], tile[slot, :, c * width:(c + 1) * width])
            for g in range(count_groups):
                keep_cols(side, phase, g, fold(product[2 * SUB * g:2 * SUB * (g + 1)]), False, c * width // LANES)

    def take(side, phase, g):
        sem = rs_r.at[side.rs0 + phase, g]

        def some(count):
            wait_bytes(side.recv.at[phase, g, pl.ds(0, count)], sem)
        some(half - 1 if side is child or SUM_AT[phase] == SUM_FROM[phase] else half)
        total = side.recv[phase, g, 0]
        for s in range(1, half):
            total = total + side.recv[phase, g, s]
        return total

    def spread(side, phase, g, value):
        at = pl.ds(side.per * chunk_of(q, g), side.per)
        ref = side.y.at[phase, g, at]
        side.y[phase, g, at] = value
        sems = (ag_s.at[side.ag0 + phase, g], ag_r.at[side.ag0 + phase, g])
        source = at_pair(side, phase, CAST_FROM)
        target = p if side is child else CAST_TO[phase][0]

        def send(i):
            remote(ref, ref, *sems, (target * half + lax.rem(q + i, half), b))
        loop(half, send, 1 if side is child or target == source else 0)

    def spread_more(phase, g):
        @pl.when(mine(root, CAST_FROM[phase], g))
        def _():
            ref = root.y.at[phase, g, pl.ds(root.per * chunk_of(q, g), root.per)]
            target = CAST_TO[phase][1]

            def send(i):
                remote(ref, ref, ag_s.at[phase, g], ag_r.at[phase, g], (target * half + lax.rem(q + i, half), b))
            loop(half, send, 1 if target == CAST_FROM[phase] else 0)

    def gather(side, phase, g):
        def some(count):
            wait_bytes(side.y.at[phase, g, pl.ds(0, side.per * count)], ag_r.at[side.ag0 + phase, g])
        both(mine(side, at_pair(side, phase, CAST_FROM), g), lambda: some(side.chunks - 1),
             lambda: some(side.chunks))
        for i in range(side.term.shape[2]):
            put(side.v, g, i, side.y[phase, g, i])

    def step(side, phase, out, g, base=None, early=None):
        @pl.when(mine(side, at_pair(side, phase, SUM_AT), g))
        def _():
            total = take(side, phase, g)
            if early is not None:
                total = total + early(g)
            if base is not None:
                total = side.y[base, g, pl.ds(side.per * chunk_of(q, g), side.per)] - total
            spread(side, out, g, total)

    lead = (b == 0).astype(jnp.float32)

    def side_rows(ref, h, g, i):
        return ref[h, aligned(g, SUB), lanes(i)]

    def put_child(g):
        for i in range(child_rb):
            put(xc, g, i, side_rows(cside, 0, g, i))
    groups(put_child)

    panel_blocks = half * root_rb

    def route(s):
        r = emap[s]
        k = lax.div(r, panel_blocks)
        within = lax.rem(r, panel_blocks)
        low = jnp.minimum(k, ROOT_PANELS - 1 - k)
        own[s] = half * low + lax.div(within, root_rb)
        place[s] = jnp.where(k == low, 0, root_rb) + lax.rem(within, root_rb)

    def invert(u):
        index = jnp.int32(0)
        tag = jnp.int32(-1)
        for s in range(sends):
            match = own[s] == u
            index = jnp.where(match, s, index)
            tag = jnp.where(match, place[s], tag)
        inv[u] = index
        tgs[u] = jnp.full((SUB, LANES), tag, jnp.int32)

    part_rows = 16
    slots = shuffle.shape[0]
    parts = gv.shape[0] // (part_rows * slots)

    def part(n):
        for s in range(slots):
            at = pl.ds(pl.multiple_of((n * slots + s) * part_rows, part_rows), part_rows)
            rows = gv[at].reshape(2 * part_rows, gv.shape[2]).astype(jnp.float32)
            for j in range(gv.shape[2] // LANES):
                shuffle[s, j] = rows[:, lanes(j)]
            for j in range(gv.shape[2] // LANES):
                for k in range(2):
                    gt[k, at, lanes(j)] = shuffle[s, j, pl.ds(k, part_rows, stride=2), :].astype(gt.dtype)

    loads_c[0].wait()
    cols_whole(child, 0, xc, ct, 0)
    loop(sends, route)
    loop(fronts, invert)
    pl.semaphore_wait(barrier, fronts - 1 + blks - 1)
    groups(lambda g: send_chunks(child, 0, g))
    tgr[f] = tgs[f]

    def send_tag(i):
        u = lax.rem(f + i, fronts)
        remote(tgs.at[u], tgr.at[f], t_s.at[0], t_r.at[0], (u, b))
    loop(fronts, send_tag, 1)
    load_g.wait()
    loop(parts // 2, part)
    groups(lambda g: step(child, 0, 0, g))
    loop(parts, part, parts // 2)
    loads_c[1].wait()
    loads_c[2].wait()

    def child_1(g):
        gather(child, 0, g)
        rows_out(child, 0, g, ct, 1, lambda i: lead * side_rows(cside, 1, g, i))
    groups(child_1)

    def update_0():
        for s in range(0, sends, 2):
            product = times_transposed(xvc[...], gt[0, s * LANES:(s + 2) * LANES])
            for g in range(count_groups):
                rows = fold(product[2 * SUB * g:2 * SUB * (g + 1)])
                for j in range(2):
                    pb[g, s + j] = rows[:, lanes(j)]
    update_0()

    def child_2(g):
        rows_in(child, 0, g)
        cols_out(child, 1, g, xc, ct, 2)
    groups(child_2)
    groups(lambda g: step(child, 1, 1, g))

    def update_1(g):
        gather(child, 1, g)
        for s in range(0, sends, 2):
            rows = fold(times_transposed(x_group(xvc, g)[...], gt[1, s * LANES:(s + 2) * LANES]))
            for j in range(2):
                pb[g, s + j] = pb[g, s + j] + rows[:, lanes(j)]
        ar[g, f] = pb[g, inv[f]]

        def send_block(i):
            u = lax.rem(f + i, fronts)
            ob[g, u] = pb[g, inv[u]]
            remote(ob.at[g, u], ar.at[g, f], x_s.at[0, g], x_r.at[0, g], (u, b))
        loop(fronts, send_block, 1)
    groups(update_1)
    for l in loads_r:
        l.wait()
    wait_bytes(tgr.at[pl.ds(0, fronts - 1)], t_r.at[0])

    def land(g):
        wait_bytes(ar.at[g, pl.ds(0, fronts - 1)], x_r.at[0, g])

        def add(u, totals):
            block = ar[g, u]
            tag = tgr[u]
            return tuple(t + jnp.where(tag == s, block, 0.0) for s, t in enumerate(totals))
        zero = jnp.zeros((SUB, LANES), jnp.float32)
        landed = lax.fori_loop(0, fronts, add, (zero,) * (2 * root_rb), unroll=16)
        for h in range(2):
            for i in range(root_rb):
                run[g, h, i] = lead * side_rows(rside, h, g, i) - landed[h * root_rb + i]

    def on(pair, body):
        pl.when(p == pair)(body)

    def subtract(slot):
        width = 2 * LANES
        for c in range(0, root_rb * LANES, width):
            size = min(width, root_rb * LANES - c)
            product = times_transposed(xv[...], rt[slot, c:c + size])
            for g in range(count_groups):
                rows = fold(product[2 * SUB * g:2 * SUB * (g + 1)])
                for j in range(size // LANES):
                    run[g, 1, c // LANES + j] = run[g, 1, c // LANES + j] - rows[:, lanes(j)]

    def solve(phase, slot):
        def one(g):
            rows_in(root, phase, g)
            cols_out(root, phase, g, xr, rt, slot)
        groups(one)

    def advance(cast, phase, h, slot):
        def one(g):
            gather(root, cast, g)
            rows_out(root, phase, g, rt, slot, lambda i: run[g, h, i])
        groups(one)

    def retreat(cast, phase, h, slot):
        def one(g):
            gather(root, cast, g)
            rows_out(root, phase, g, rt, slot)
        groups(one)

    def finish(phase, h, after):
        def one(g):
            def use(i, v):
                zb[g, h * root_rb + i] = v
                rout[h, aligned(g, SUB), lanes(i)] = v
            rows_in(root, phase, g, use)
            after(g)
        groups(one)

    def answers(g):
        def answer(u):
            tag = tgr[u]
            block = jnp.where(tag == 0, zb[g, 0], 0.0)
            for s in range(1, 2 * root_rb):
                block = jnp.where(tag == s, zb[g, s], block)
            return block

        def send_answer(i):
            u = lax.rem(f + i, fronts)
            rk[g, u] = answer(u)
            remote(rk.at[g, u], ak.at[g, f], x_s.at[1, g], x_r.at[1, g], (u, b))
        loop(fronts, send_answer, 1)
        ak[g, f] = answer(f)

    def first(g):
        land(g)

        @pl.when(p == 0)
        def _():
            for i in range(root_rb):
                rows_r[0, g, b, i] = run[g, 0, i]
            send_rows(root, 0, g)
    groups(first)

    def relay(index, g, value, peer):
        relay_out[index, g] = value
        remote(relay_out.at[index, g], relay_in.at[index, g], relay_s.at[index, g], relay_r.at[index, g], (peer, b))

    def relayed(index, g):
        wait_bytes(relay_in.at[index, g], relay_r.at[index, g])
        return relay_in[index, g]

    def relay_y(g):
        @pl.when(mine(root, 1, g))
        def _():
            relay(0, g, root.y[1, g, pl.ds(root.per * chunk_of(q, g), root.per)], f - half)

    def spread_y(g):
        @pl.when(mine(root, 0, g))
        def _():
            spread(root, AGAIN_1, g, relayed(0, g))

    def relay_sum(g):
        @pl.when(mine(root, 0, g))
        def _():
            relay(1, g, take(root, EARLY_1, g), f + half)

    def links_free(index, peer):
        pl.semaphore_signal(free.at[index], inc=1, device_id=(peer, b), device_id_type=MESH)

    @functools.partial(on, 0)
    def _():
        solve(0, 0)
        groups(lambda g: step(root, 0, 0, g))
        pl.semaphore_wait(free.at[0], 1)
        groups(lambda g: spread_more(0, g))
        groups(lambda g: gather(root, 0, g))
        subtract(1)
        groups(spread_y)
        groups(lambda g: gather(root, AGAIN_1, g))
        subtract(2)
        advance(2, 3, 1, 3)
        solve(3, 4)
        groups(lambda g: step(root, 3, 3, g))
        retreat(3, 4, 1, 4)
        finish(4, 1, lambda g: cols_out(root, BACK_2, g, xr, rt, 3))
        cols_whole(root, EARLY_1, xr, rt, 2)
        cols_whole(root, EARLY_0, xr, rt, 1)
        pl.semaphore_wait(free.at[1], 1)
        groups(lambda g: send_chunks(root, EARLY_1, g))
        groups(lambda g: send_chunks(root, EARLY_0, g))
        groups(relay_sum)
        groups(lambda g: step(root, BACK_0, 6, g, base=0, early=lambda g: take(root, EARLY_0, g)))
        links_free(2, f + half)
        retreat(6, 7, 0, 0)
        finish(7, 0, lambda g: answers(g))

    @functools.partial(on, 1)
    def _():
        advance(0, 1, 0, 0)
        links_free(0, f - half)
        subtract(2)
        solve(1, 1)
        groups(lambda g: step(root, 1, 1, g))
        advance(1, 2, 1, 3)
        groups(relay_y)
        solve(2, 4)
        groups(lambda g: step(root, 2, 2, g))
        groups(lambda g: step(root, BACK_2, 4, g, base=2))
        links_free(1, f - half)
        retreat(4, 5, 1, 4)
        finish(5, 1, lambda g: cols_out(root, BACK_1, g, xr, rt, 3))
        cols_whole(root, BACK_0, xr, rt, 2)
        groups(lambda g: step(root, BACK_1, 5, g, base=1, early=lambda g: relayed(1, g)))
        retreat(5, 6, 0, 1)
        finish(6, 0, lambda g: cols_out(root, BACK_0, g, xr, rt, 0, add=True))
        pl.semaphore_wait(free.at[2], 1)
        groups(lambda g: answers(g))

    def drain_terms(side, phase, g, same):
        def some(count):
            wait_bytes(side.term.at[phase, g, pl.ds(0, side.per * count)], rs_s.at[side.rs0 + phase, g])
        if same:
            both(mine(side, at_pair(side, phase, SUM_AT), g), lambda: some(side.chunks - 1), lambda: some(side.chunks))
        else:
            some(side.chunks)

    def drain_rows(side, phase, g):
        wait_bytes(side.rows.at[phase, g, pl.ds(0, blks - 1)], blk_s.at[side.blk0 + phase, g])

    def drain_root(g):
        for pair in range(2):
            @functools.partial(on, pair)
            def _(pair=pair):
                for phase, source in enumerate(SUM_FROM):
                    if source == pair:
                        drain_terms(root, phase, g, SUM_AT[phase] == pair)
                for phase, source in enumerate(ROOT_ROWS):
                    if source == pair:
                        drain_rows(root, phase, g)

                @pl.when(mine(root, pair, g))
                def _():
                    wait_bytes(relay_out.at[1 - pair, g], relay_s.at[1 - pair, g])
                    for phase, source in enumerate(CAST_FROM):
                        if source == pair:
                            count = half * len(CAST_TO[phase]) - (source in CAST_TO[phase])
                            wait_bytes(counts.at[pl.ds(0, count)], ag_s.at[phase, g])

    def drain_child(g, sums, rows):
        for phase in sums:
            drain_terms(child, phase, g, True)
        for phase in rows:
            drain_rows(child, phase, g)

        @pl.when(mine(child, None, g))
        def _():
            for phase in sums:
                wait_bytes(recv_c.at[phase, g, pl.ds(0, half - 1)], ag_s.at[child.ag0 + phase, g])

    def child_3(g):
        wait_bytes(ak.at[g, pl.ds(0, fronts - 1)], x_r.at[1, g])

        def keep(u):
            nk[u] = ak[g, u]
        loop(fronts, keep)
        for s in range(sends):
            put(xn, g, s, nk[own[s]])
        cols_out(child, 2, g, xn, gt, 1)
    groups(child_3)
    cols_whole(child, 3, xn, gt, 0)
    groups(drain_root)
    groups(lambda g: step(child, 2, 2, g, base=1))

    def child_4(g):
        gather(child, 2, g)
        rows_out(child, 1, g, ct, 2)
    groups(child_4)

    def last(h, g):
        def use(i, v):
            cout[h, aligned(g, SUB), lanes(i)] = v
        return use

    def child_5(g):
        rows_in(child, 1, g, last(1, g))
        cols_out(child, 3, g, xc, ct, 1, add=True)
    groups(child_5)

    def drain_early(g):
        drain_child(g, (0, 1), (0, 1))
        wait_bytes(ob.at[g, pl.ds(0, fronts - 1)], x_s.at[0, g])
        wait_bytes(rk.at[g, pl.ds(0, fronts - 1)], x_s.at[1, g])
    groups(drain_early)
    wait_bytes(tgs.at[pl.ds(0, fronts - 1)], t_s.at[0])
    groups(lambda g: step(child, 3, 3, g, base=0))
    groups(lambda g: drain_child(g, (2,), ()))

    def child_6(g):
        gather(child, 3, g)
        rows_out(child, 2, g, ct, 0)
    groups(child_6)
    groups(lambda g: rows_in(child, 2, g, last(0, g)))

    groups(lambda g: drain_child(g, (3,), (2,)))

def place_fields(root_in, child_in, root_out, child_out):
    root_out[0] = root_in[...]
    child_out[0] = child_in[...]


def on_device(fronts, blks, root_tiles, child_tiles, child_update, extend_map, root_side, child_side):
    root, child = root_tiles[0], child_tiles[0]
    rside, cside = root_side[0], child_side[0]
    directions = rside.shape[1]
    groups = directions // SUB
    half = fronts // 2
    root_rb, child_rb = rside.shape[2] // LANES, cside.shape[2] // LANES
    root_cols, child_cols = root.shape[2], child.shape[2]
    root_blocks, child_blocks = root_cols // LANES, child_cols // LANES
    update_rows, panels, _ = child_update.shape
    sends = extend_map.shape[0]
    root_per = -(-root_blocks // half)
    child_per = -(-child_blocks // half)
    f32, bf16 = jnp.float32, jnp.bfloat16
    vmem, sem = pltpu.VMEM, pltpu.SemaphoreType.DMA
    sums, rows, casts = len(SUM_FROM), len(ROOT_ROWS), len(CAST_FROM)
    whole = pl.BlockSpec(memory_space=pltpu.VMEM)
    hbm = pl.BlockSpec(memory_space=pl.ANY)
    tile = (SUB, LANES)
    outs = pl.pallas_call(
        functools.partial(kernel, fronts, blks),
        out_shape=(jax.ShapeDtypeStruct(rside.shape, f32), jax.ShapeDtypeStruct(cside.shape, f32)),
        in_specs=[pl.BlockSpec(memory_space=pltpu.SMEM), whole, whole, hbm, hbm, hbm],
        out_specs=(whole, whole),
        scratch_shapes=[
            vmem(root.shape, bf16), vmem(child.shape, bf16), vmem(child_update.shape, bf16),
            vmem((panels, update_rows, child_cols), bf16), vmem((4, child_blocks, 32, LANES), f32),
            vmem((groups, 2, root_rb) + tile, f32),
            vmem((2 * directions, rside.shape[2]), bf16), vmem((2 * directions, root_cols), bf16),
            vmem((2 * directions, cside.shape[2]), bf16), vmem((2 * directions, child_cols), bf16),
            vmem((2 * directions, sends * LANES), bf16),
            vmem((groups, sends) + tile, f32),
            vmem((groups, fronts) + tile, f32), vmem((groups, fronts) + tile, f32),
            vmem((groups, fronts) + tile, f32), vmem((groups, fronts) + tile, f32),
            vmem((fronts,) + tile, f32),
            vmem((fronts,) + tile, jnp.int32), vmem((fronts,) + tile, jnp.int32),
            vmem((groups, 2 * root_rb) + tile, f32),
            vmem((rows, groups, blks, root_rb) + tile, f32), vmem((sums, groups, root_blocks) + tile, f32),
            vmem((sums, groups, half, root_per) + tile, f32), vmem((casts, groups, root_blocks) + tile, f32),
            vmem((CHILD_ROWS, groups, blks, child_rb) + tile, f32),
            vmem((CHILD_SUMS, groups, child_blocks) + tile, f32),
            vmem((CHILD_SUMS, groups, half, child_per) + tile, f32),
            vmem((CHILD_SUMS, groups, child_blocks) + tile, f32),
            vmem((fronts, root_per) + tile, f32),
            vmem((2, groups, root_per) + tile, f32), vmem((2, groups, root_per) + tile, f32),
            pltpu.SMEM((sends,), jnp.int32), pltpu.SMEM((sends,), jnp.int32),
            pltpu.SMEM((fronts,), jnp.int32),
            sem((4 + root.shape[0],)),
            sem((rows + CHILD_ROWS, groups)), sem((rows + CHILD_ROWS, groups)),
            sem((sums + CHILD_SUMS, groups)), sem((sums + CHILD_SUMS, groups)),
            sem((casts + CHILD_SUMS, groups)), sem((casts + CHILD_SUMS, groups)),
            sem((2, groups)), sem((2, groups)), sem((1,)), sem((1,)),
            sem((2, groups)), sem((2, groups)),
            pltpu.SemaphoreType.REGULAR((3,)),
        ],
        compiler_params=pltpu.CompilerParams(
            collective_id=0, has_side_effects=True, vmem_limit_bytes=58 * 1024 * 1024
        ),
    )(extend_map, rside, cside, root, child, child_update)
    outs = pl.pallas_call(
        place_fields,
        out_shape=tuple(jax.ShapeDtypeStruct((1,) + o.shape, f32) for o in outs),
        in_specs=[whole, whole], out_specs=(whole, whole),
    )(*outs)
    return tuple(outs)


def solution(mesh):
    in_specs = (
        P("front", None, None, "blk"),
        P("front", None, None, "blk"),
        P("front", None, "blk"),
        P("front"),
        P("front", None, None, None),
        P("front", None, None, None),
    )
    out_specs = (P("front", None, None, None), P("front", None, None, None))
    body = functools.partial(on_device, mesh.shape["front"], mesh.shape["blk"])
    return jax.shard_map(body, mesh=mesh, in_specs=in_specs, out_specs=out_specs, check_vma=False)
```
